32 devices in a mesh: pipe: 2 (over y), dp: 8 (over z, x), tensor: 2 (over core).
Axes of the slice: x: 2, y: 2, z: 4, core: 2. Of those that a mesh axis runs over, the one named last changes fastest.
Arguments:
- inputs: bfloat16 [2, 1536, 768], P(None, ('dp', 'tensor')), may hold values from -6 to 6
- lengths: int32 [2, 8, 3], P(None, 'dp'), may hold values from 1 to 144, 192 in all within a row
- ln1_gain: bfloat16 [2, 768], P('pipe', 'dp'), may hold values from 0.25 to 1.75
- ln1_shift: bfloat16 [2, 768], P('pipe', 'dp'), may hold values from -1.5 to 1.5
- ln2_gain: bfloat16 [2, 768], P('pipe', 'dp'), may hold values from 0.25 to 1.75
- ln2_shift: bfloat16 [2, 768], P('pipe', 'dp'), may hold values from -1.5 to 1.5
- qkv_weight: bfloat16 [2, 768, 2304], P('pipe', 'dp', 'tensor'), may hold values from -0.21875 to 0.21875
- qkv_bias: bfloat16 [2, 2304], P('pipe', 'tensor'), may hold values from -2.5 to 2.5
- out_weight: bfloat16 [2, 768, 768], P('pipe', 'tensor', 'dp'), may hold values from -1 to 1
- fc_weight: bfloat16 [2, 768, 3072], P('pipe', 'dp', 'tensor'), may hold values from -0.21875 to 0.21875
- fc_bias: bfloat16 [2, 3072], P('pipe', 'tensor'), may hold values from -2.5 to 2.5
- proj_weight: bfloat16 [2, 3072, 768], P('pipe', 'tensor', 'dp'), may hold values from -0.109375 to 0.109375
- branch_bias: bfloat16 [2, 768], P('pipe', 'dp'), may hold values from -1.5 to 1.5
- cotangent: bfloat16 [2, 1536, 768], P(None, ('dp', 'tensor')), may hold values from -6 to 6
Outputs:
- activations: bfloat16 [2, 2, 1536, 768], P('pipe', None, ('dp', 'tensor'))
- input_grads: bfloat16 [2, 2, 1536, 768], P('pipe', None, ('dp', 'tensor'))
- ln1_gain_grad: float32 [2, 768], P('pipe', 'dp')
- ln1_shift_grad: float32 [2, 768], P('pipe', 'dp')
- ln2_gain_grad: float32 [2, 768], P('pipe', 'dp')
- ln2_shift_grad: float32 [2, 768], P('pipe', 'dp')
- qkv_weight_grad: float32 [2, 768, 2304], P('pipe', 'dp', 'tensor')
- qkv_bias_grad: float32 [2, 2304], P('pipe', 'tensor')
- out_weight_grad: float32 [2, 768, 768], P('pipe', 'tensor', 'dp')
- fc_weight_grad: float32 [2, 768, 3072], P('pipe', 'dp', 'tensor')
- fc_bias_grad: float32 [2, 3072], P('pipe', 'tensor')
- proj_weight_grad: float32 [2, 3072, 768], P('pipe', 'tensor', 'dp')
- branch_bias_grad: float32 [2, 768], P('pipe', 'dp')
The draws below stay inside these ranges and needn't reach their ends.
Inputs may be any that keep to these rules, and one draw needn't show every extreme that they name: Each row holds, in order, the lengths of the 3 sequences that fill one group's 192 rows of a micro-batch; they sum to 192, and the longest of each row is exactly 144.
All inputs are finite; a program needn't handle non-finite values.
Results may differ from the reference program's by a relative error of at most 0.017.
Values may be sent and summed in bfloat16 or wider, within the bound.
No kernel may reach another device: no remote copies, remote signals or barrier semaphores. Data moves between devices by JAX's collectives and lax.ppermute only.
A program may use at most 128 MiB of HBM per device.

```python
import math
import jax
import jax.numpy as jnp
import numpy as np
from jax import lax

D = 768
HEADS = 12
HEAD = 64
ROT = 16
FF = 3072
MICRO = 2
NSEQ = 3
GROUP = 192
TOKS = 1536
LONGEST = 144
N_PIPE = 2
N_DP = 8


def raised(result, rng, source, target, parts, factor):
    owner, partner = [(jnp.arange(result.shape[position]) // (result.shape[position] // parts)).reshape([-1 if axis == position else 1 for axis in range(result.ndim)]) for position in (source, target)]
    chosen = jax.random.permutation(rng, parts)[partner]
    strong = (owner == chosen) | (owner == (partner + parts // 2) % parts)
    return jnp.where(strong, factor * result, result)


def level_of(stream_key, dims, cuts, low, top_value):
    loudness, own = 1.0, jax.random.fold_in(stream_key, 6)
    for dim, parts in cuts:
        heights = jnp.exp(jax.random.uniform(jax.random.fold_in(own, dim), (parts,), jnp.float32, low / len(cuts), top_value / len(cuts)))
        loudness = loudness * jnp.repeat(heights, dims[dim] // parts).reshape([-1 if axis == dim else 1 for axis in range(len(dims))])
    return loudness


def split_up(amount, total, bound, lean):
    weights = [(1 << 20) // math.isqrt(standing ** lean) + 1 for standing in range(2, amount + 1)]
    surplus, counts = total - bound - (amount - 1), [1] * (amount - 1)
    while surplus > 0:
        free = [i for i in range(amount - 1) if counts[i] < bound]
        mass, left = sum([weights[i] for i in free]), surplus
        for i in free:
            more = min(bound - counts[i], max(1, left * weights[i] // mass), surplus)
            counts[i] = counts[i] + more
            surplus = surplus - more
    return np.array([bound] + counts)


def ragged(stream_key, number_of, total, limit, skew):
    if number_of == 2:
        one = jax.random.randint(stream_key, (), max(1, total - limit), min(limit, total - 1) + 1)
        return jnp.stack([one, total - one])
    sizes = jnp.asarray(split_up(number_of, total, limit, skew), jnp.int32)
    twos = (number_of - 1) // 2
    donor, sink = sizes[1:1 + 2 * twos:2], sizes[2:2 + 2 * twos:2]
    slack = jnp.minimum(donor - 1, limit - sink)
    shifted = jax.random.randint(jax.random.fold_in(stream_key, 1), (twos,), 0, 1 << 20) % (slack + 1)
    sizes = sizes.at[1:1 + 2 * twos:2].set(donor - shifted).at[2:2 + 2 * twos:2].set(sink + shifted)
    return sizes[jax.random.permutation(jax.random.fold_in(stream_key, 2), number_of)]


def bell_draw(rng, extent, deviation, most, pieces=(), kind=jnp.bfloat16):
    entries = jax.random.normal(rng, extent, jnp.float32) * deviation
    if len(pieces) > 0:
        entries = level_of(rng, extent, pieces, -0.22, 0.18) * entries
    return jnp.clip(entries, min=-most, max=most).astype(kind)


def heavy_noise(rng, extent, scale, bound, cuts, heavy, held_as=jnp.bfloat16):
    values = scale * jax.random.normal(rng, extent, jnp.float32)
    if cuts:
        values = values * level_of(rng, extent, cuts, -0.22, 0.18)
    return jnp.clip(raised(values, jax.random.fold_in(rng, 3), *heavy), -bound, bound).astype(held_as)


def setup_inputs(seed: int = 0) -> dict:
    streams_of = jax.random.split(jax.random.key(seed), 15)
    inputs = bell_draw(streams_of[0], (MICRO, TOKS, D), 1.0, 6.0, ((1, 16),))
    lengths = jax.vmap(lambda own: ragged(own, NSEQ, GROUP, LONGEST, 2))(jax.random.split(streams_of[1], MICRO * N_DP)).reshape((MICRO, N_DP, NSEQ)).astype(jnp.int32)
    ln1_gain = jnp.clip(1.0 + 0.15 * jax.random.normal(streams_of[2], (N_PIPE, D), jnp.float32), 0.25, 1.75).astype(jnp.bfloat16)
    ln1_shift = bell_draw(streams_of[3], (N_PIPE, D), 0.3, 1.5, ((0, 2), (1, 8)))
    ln2_gain = jnp.clip(1.0 + 0.15 * jax.random.normal(streams_of[4], (N_PIPE, D), jnp.float32), 0.25, 1.75).astype(jnp.bfloat16)
    ln2_shift = bell_draw(streams_of[5], (N_PIPE, D), 0.3, 1.5, ((0, 2), (1, 8)))
    qkv_weight = bell_draw(streams_of[6], (N_PIPE, D, 3 * D), D ** -0.5, 0.21875, ((0, 2), (1, 8), (2, 2)))
    qkv_bias = bell_draw(streams_of[7], (N_PIPE, 3 * D), 0.5, 2.5, ((0, 2), (1, 2)))
    out_weight = bell_draw(streams_of[8], (N_PIPE, D, D), (HEAD // 2) ** -0.5, 1.0, ((0, 2), (1, 2), (2, 8)))
    fc_weight = bell_draw(streams_of[9], (N_PIPE, D, FF), D ** -0.5, 0.21875, ((0, 2), (1, 8), (2, 2)))
    fc_bias = bell_draw(streams_of[10], (N_PIPE, FF), 0.5, 2.5, ((0, 2), (1, 2)))
    proj_weight = bell_draw(streams_of[11], (N_PIPE, FF, D), FF ** -0.5, 0.109375, ((0, 2), (1, 2), (2, 8)))
    branch_bias = bell_draw(streams_of[12], (N_PIPE, D), 0.3, 1.5, ((0, 2), (1, 8)))
    cotangent = heavy_noise(streams_of[13], (MICRO, TOKS, D), 1.0, 6.0, ((1, 16),), (1, 2, 16, 2.0))
    return {"inputs": inputs, "lengths": lengths, "ln1_gain": ln1_gain, "ln1_shift": ln1_shift, "ln2_gain": ln2_gain, "ln2_shift": ln2_shift, "qkv_weight": qkv_weight, "qkv_bias": qkv_bias, "out_weight": out_weight, "fc_weight": fc_weight, "fc_bias": fc_bias, "proj_weight": proj_weight, "branch_bias": branch_bias, "cotangent": cotangent}


@jax.custom_vjp
def low(v):
    return lax.optimization_barrier(v.astype(jnp.bfloat16)).astype(jnp.float32)

@jax.custom_vjp
def low_back(v):
    return v

def low_keep(v):
    return (low(v), None)

def low_pass(kept, grad):
    return (grad,)

def back_keep(v):
    return (v, None)

def back_low(kept, grad):
    return (low(grad),)
low.defvjp(low_keep, low_pass)
low_back.defvjp(back_keep, back_low)
EPSILON = 1e-05
NEG_BIG = -1e+30
HIGHEST = lax.Precision.HIGHEST

def layer_norm(values, gain, offset):
    average = lax.optimization_barrier(jnp.mean(values, axis=-1, keepdims=True))
    centred = values - average
    spread = lax.optimization_barrier(jnp.mean(centred * centred, axis=-1, keepdims=True))
    return centred * lax.rsqrt(spread + EPSILON) * gain + offset

def sequence_layout(seq_lengths, row_count, seq_count):
    seq_ends = jnp.cumsum(seq_lengths).astype(jnp.int32)
    places = jnp.arange(row_count, dtype=jnp.int32)
    segment = lax.optimization_barrier(jnp.sum((places[:, None] >= seq_ends[None, :]).astype(jnp.int32), axis=1))
    seq_starts = seq_ends - seq_lengths
    picked = segment[:, None] == jnp.arange(seq_count, dtype=jnp.int32)[None, :]
    first_row = lax.optimization_barrier(jnp.sum(jnp.where(picked, seq_starts[None, :], 0), axis=1)).astype(jnp.int32)
    return (segment, places - first_row)

def layout_block(seq_lengths):
    return sequence_layout(seq_lengths, GROUP, NSEQ)

def rotary_tables(positions, rot_dims):
    half_dims = rot_dims // 2
    counter = jnp.arange(half_dims, dtype=jnp.float32)
    inverse = jnp.exp(counter * (-2.0 * math.log(10000.0) / rot_dims))
    angles = positions.astype(jnp.float32)[..., None] * inverse
    angles = jnp.concatenate([angles, angles], axis=-1)
    return (jnp.cos(angles), jnp.sin(angles))

def apply_rotary(heads, cosine, sine):
    rot_dims = cosine.shape[-1]
    half_dims = rot_dims // 2
    front = heads[..., :rot_dims]
    turned = jnp.concatenate([-front[..., half_dims:], front[..., :half_dims]], axis=-1)
    front = front * cosine[..., None, :] + turned * sine[..., None, :]
    return jnp.concatenate([front, heads[..., rot_dims:]], axis=-1)

def attend_block(queries, key_rows, value_rows, segment):
    row_ids = jnp.arange(segment.shape[0], dtype=jnp.int32)
    allowed = (segment[:, None] == segment[None, :]) & (row_ids[:, None] >= row_ids[None, :])
    scores = jnp.einsum('qhd,khd->hqk', queries, key_rows, precision=HIGHEST) * (1.0 / math.sqrt(HEAD))
    scores = low_back(scores)
    scores = jnp.where(allowed[None], scores, NEG_BIG)
    row_peak = lax.optimization_barrier(jnp.max(scores, axis=-1, keepdims=True))
    expons = jnp.exp(scores - row_peak)
    attn_weights = low(expons / lax.optimization_barrier(jnp.sum(expons, axis=-1, keepdims=True)))
    return jnp.einsum('hqk,khd->qhd', attn_weights, value_rows, precision=HIGHEST)

def attend_items(items):
    return attend_block(items[0], items[1], items[2], items[3])

def section_layer(hidden, segment, cosine, sine, weights):
    gain_one, shift_one, gain_two, shift_two, qkv_matrix, qkv_offset, out_matrix, fc_matrix, fc_offset, proj_matrix, branch_offset = weights
    blocks, row_count, width = hidden.shape
    first = low(layer_norm(hidden, gain_one, shift_one))
    second = low(layer_norm(hidden, gain_two, shift_two))
    packed = jnp.einsum('bgd,de->bge', first, qkv_matrix, precision=HIGHEST) + qkv_offset
    packed = low_back(packed).reshape(blocks, row_count, HEADS, 3, HEAD)
    queries = low(apply_rotary(packed[:, :, :, 0], cosine, sine))
    key_rows = low(apply_rotary(packed[:, :, :, 1], cosine, sine))
    value_rows = low(packed[:, :, :, 2])
    mixed = lax.map(jax.checkpoint(attend_items), (queries, key_rows, value_rows, segment))
    mixed = low_back(low(mixed.reshape(blocks, row_count, width)))
    pre_act = jnp.einsum('bgd,df->bgf', second, fc_matrix, precision=HIGHEST) + fc_offset
    pre_act = low_back(pre_act)
    hidden_act = low(jax.nn.gelu(pre_act, approximate=False))
    branches = jnp.einsum('bgd,de->bge', mixed, out_matrix, precision=HIGHEST)
    branches = branches + jnp.einsum('bgf,fe->bge', hidden_act, proj_matrix, precision=HIGHEST)
    return hidden + branches + branch_offset

def reference(inputs, lengths, ln1_gain, ln1_shift, ln2_gain, ln2_shift, qkv_weight, qkv_bias, out_weight, fc_weight, fc_bias, proj_weight, branch_bias, cotangent):
    blocks = MICRO * N_DP
    seq_lengths = lengths.reshape(blocks, NSEQ).astype(jnp.int32)
    segment, positions = jax.vmap(layout_block)(seq_lengths)
    cosine, sine = rotary_tables(positions, ROT)
    params = tuple((item.astype(jnp.float32) for item in (ln1_gain, ln1_shift, ln2_gain, ln2_shift, qkv_weight, qkv_bias, out_weight, fc_weight, fc_bias, proj_weight, branch_bias)))
    start_rows = inputs.astype(jnp.float32).reshape(blocks, GROUP, D)
    nudge_rows = jnp.zeros_like(start_rows)

    def forward(section_input, nudge_input, *section_params):
        section_zero = tuple((item[0] for item in section_params))
        section_one = tuple((item[1] for item in section_params))
        middle = low_back(low(section_layer(section_input, segment, cosine, sine, section_zero)) + nudge_input)
        final = section_layer(middle, segment, cosine, sine, section_one)
        return (middle, final)
    (middle, final), pullback = jax.vjp(forward, start_rows, nudge_rows, *params)
    grads = pullback((jnp.zeros_like(middle), cotangent.astype(jnp.float32).reshape(blocks, GROUP, D)))
    activations = jnp.stack([middle, final]).astype(jnp.bfloat16).reshape(N_PIPE, MICRO, TOKS, D)
    input_grads = jnp.stack([grads[0], grads[1]]).astype(jnp.bfloat16).reshape(N_PIPE, MICRO, TOKS, D)
    return (activations, input_grads, grads[2], grads[3], grads[4], grads[5], grads[6], grads[7], grads[8], grads[9], grads[10], grads[11], grads[12])
```

```python
import functools
import math

import jax
import jax.numpy as jnp
from jax import lax
from jax.experimental import pallas as pl
from jax.experimental.pallas import tpu as pltpu
from jax.sharding import PartitionSpec as P

HEAD = 64
ROT = 16
EPSILON = 1e-05
NEG_BIG = -1e30
VMEM_LIMIT = 48 * 1024 * 1024
BF = jnp.bfloat16
F32 = jnp.float32
SMALL = 128


def ring_device(place, count):
    if count == 8:
        return jnp.where(place < 4, 2 * place, 15 - 2 * place)
    if count == 32:
        folded = jnp.where(place < 16, place, 31 - place)
        row, column = folded // 4, folded % 4
        column = jnp.where(row % 2 == 0, column, 3 - column)
        return row * 4 + column + jnp.where(place < 16, 0, 16)
    return place


def ring_place(device, count):
    if count == 8:
        half = device // 2
        return jnp.where(device % 2 == 0, half, 7 - half)
    if count == 32:
        within = device % 16
        row, column = within // 4, within % 4
        column = jnp.where(row % 2 == 0, column, 3 - column)
        folded = row * 4 + column
        return jnp.where(device < 16, folded, 31 - folded)
    return device


def ring_list(count):
    if count == 8:
        return [0, 2, 4, 6, 7, 5, 3, 1]
    if count == 32:
        snake = []
        for row in range(4):
            line = [row * 4 + column for column in range(4)]
            snake += line if row % 2 == 0 else line[::-1]
        return snake + [16 + item for item in reversed(snake)]
    return list(range(count))


def ring_routes(count):
    order = ring_list(count)
    ahead = [(order[i], order[(i + 1) % count]) for i in range(count)]
    return ahead, [(target, source) for source, target in ahead]


def ring_gather(chunk, forward_steps):
    count = lax.axis_size("dp")
    ahead, behind = ring_routes(count)
    me = lax.axis_index("dp")
    place = ring_place(me, count)
    depth, width = chunk.shape
    whole = jnp.zeros((count * depth, width), chunk.dtype)
    whole = lax.dynamic_update_slice(whole, chunk, (me * depth, 0))
    backward_steps = count - 1 - forward_steps
    front = back = chunk
    for step in range(1, max(forward_steps, backward_steps) + 1):
        if step <= forward_steps:
            front = lax.ppermute(front, "dp", ahead)
            owner = ring_device((place + count - step) % count, count)
            whole = lax.dynamic_update_slice(whole, front, (owner * depth, 0))
        if step <= backward_steps:
            back = lax.ppermute(back, "dp", behind)
            owner = ring_device((place + step) % count, count)
            whole = lax.dynamic_update_slice(whole, back, (owner * depth, 0))
    return whole


def ring_scatter(terms, forward_steps):
    count = lax.axis_size("dp")
    ahead, behind = ring_routes(count)
    place = ring_place(lax.axis_index("dp"), count)
    depth = terms.shape[0] // count
    backward_steps = count - 1 - forward_steps

    def term(distance):
        owner = ring_device((place + count + distance) % count, count)
        return lax.dynamic_slice(terms, (owner * depth, 0), (depth, terms.shape[1]))

    front = back = None
    for step in range(max(forward_steps, backward_steps)):
        if step < forward_steps:
            own = term(forward_steps - step)
            if front is not None:
                own = (own.astype(F32) + front.astype(F32)).astype(BF)
            front = lax.ppermute(own, "dp", ahead)
        if step < backward_steps:
            own = term(step - backward_steps)
            if back is not None:
                own = (own.astype(F32) + back.astype(F32)).astype(BF)
            back = lax.ppermute(own, "dp", behind)
    return term(0).astype(F32) + front.astype(F32) + back.astype(F32)


def swap(block, axis):
    return lax.ppermute(block, axis, [(0, 1), (1, 0)])


def dot(left, right):
    return jnp.dot(left, right, preferred_element_type=F32)


def dot_last(left, right):
    return lax.dot_general(left, right, (((1,), (1,)), ((), ())), preferred_element_type=F32)


def dot_first(left, right):
    return lax.dot_general(left, right, (((0,), (0,)), ((), ())), preferred_element_type=F32)


def softmax_rows(queries, keys, bias):
    scores = dot_last(queries, keys) * (1.0 / math.sqrt(HEAD)) + bias
    peak = jnp.max(scores, axis=-1, keepdims=True)
    expons = jnp.exp(scores - peak)
    return expons / jnp.sum(expons, axis=-1, keepdims=True)


def head_parts(packed, index):
    base = index * 3 * HEAD
    return tuple(packed[:, base + j * HEAD : base + (j + 1) * HEAD] for j in range(3))


def turn(values, cosine, upper, lower):
    width = values.shape[1]
    return (
        values * cosine
        + pltpu.roll(values, width - ROT // 2, 1) * upper
        + pltpu.roll(values, ROT // 2, 1) * lower
    )


def forward_kernel(
    heads,
    own_ref,
    far_ref,
    first_w_ref,
    second_w_ref,
    qkv_bias_ref,
    fc_bias_ref,
    cos_ref,
    upper_ref,
    lower_ref,
    bias_ref,
    mine_ref,
    other_ref,
    norm1_ref,
    norm2_ref,
    xhat_ref,
    scale_ref,
    packed_ref,
    mixed_ref,
    pre_ref,
    act_ref,
    vector_ref,
):
    rows = own_ref.shape[0]
    qkv_width = heads * 3 * HEAD
    out_width = heads * HEAD
    wide = cos_ref.shape[1]
    hidden = fc_bias_ref.shape[1]
    small = first_w_ref[:, qkv_width + out_width :].astype(F32)
    vectors = jnp.transpose(small)[:8]
    vector_ref[...] = vectors
    values = jnp.concatenate([own_ref[...], far_ref[...]], axis=0).astype(F32)
    centred = values - jnp.mean(values, axis=-1, keepdims=True)
    scale = lax.rsqrt(jnp.mean(centred * centred, axis=-1, keepdims=True) + EPSILON)
    xhat = centred * scale
    xhat_ref[...] = xhat
    scale_ref[...] = jnp.broadcast_to(scale, scale_ref.shape)
    first = (xhat * vectors[0:1] + vectors[1:2]).astype(BF)
    second = (xhat * vectors[2:3] + vectors[3:4]).astype(BF)
    norm1_ref[...] = first
    norm2_ref[...] = second
    packed = dot(first, first_w_ref[:, :wide]) + qkv_bias_ref[...]
    packed = turn(packed, cos_ref[...], upper_ref[...], lower_ref[...]).astype(BF)
    packed_ref[...] = packed
    bias = bias_ref[...]
    mixed = []
    for index in range(heads):
        queries, keys, held = head_parts(packed, index)
        weights = softmax_rows(queries, keys, bias).astype(BF)
        mixed.append(dot(weights, held))
    mixed = jnp.concatenate(mixed, axis=1).astype(BF)
    mixed_ref[...] = mixed
    pre = dot(second, second_w_ref[:, :hidden]) + fc_bias_ref[...]
    pre_ref[...] = pre
    act = (pre * (0.5 + 0.5 * lax.erf(pre * math.sqrt(0.5)))).astype(BF)
    act_ref[...] = act
    total = dot_last(act, second_w_ref[:, hidden:])
    total = total + dot_last(mixed, first_w_ref[:, qkv_width : qkv_width + out_width])
    mine_ref[...] = total[:rows]
    other_ref[...] = total[rows:]


def backward_kernel(
    heads,
    own_ref,
    far_ref,
    first_w_ref,
    second_w_ref,
    cos_ref,
    upper_ref,
    lower_ref,
    bias_ref,
    xhat_ref,
    scale_ref,
    packed_ref,
    pre_ref,
    vector_ref,
    mine_ref,
    other_ref,
    d_packed_ref,
    d_pre_ref,
    sums_ref,
):
    rows = own_ref.shape[0]
    qkv_width = heads * 3 * HEAD
    out_width = heads * HEAD
    wide = cos_ref.shape[1]
    hidden = pre_ref.shape[1]
    grad = jnp.concatenate([own_ref[...], far_ref[...]], axis=0)
    d_act = dot(grad, second_w_ref[:, hidden:])
    pre = pre_ref[...]
    slope = 0.5 + 0.5 * lax.erf(pre * math.sqrt(0.5))
    slope = slope + pre * (jnp.exp(pre * pre * -0.5) * (1.0 / math.sqrt(2.0 * math.pi)))
    d_pre = (d_act * slope).astype(BF)
    d_pre_ref[...] = d_pre
    d_second = dot_last(d_pre, second_w_ref[:, :hidden])
    d_mixed = dot(grad, first_w_ref[:, qkv_width : qkv_width + out_width]).astype(BF)
    bias = bias_ref[...]
    packed = packed_ref[...]
    parts = []
    for index in range(heads):
        queries, keys, held = head_parts(packed, index)
        weights = softmax_rows(queries, keys, bias)
        given = d_mixed[:, index * HEAD : (index + 1) * HEAD]
        d_held = dot_first(weights.astype(BF), given)
        d_weights = dot_last(given, held)
        row_dot = jnp.sum(weights * d_weights, axis=-1, keepdims=True)
        d_scores = (weights * (d_weights - row_dot)).astype(BF)
        parts.append(dot(d_scores, keys) * (1.0 / math.sqrt(HEAD)))
        parts.append(dot_first(d_scores, queries) * (1.0 / math.sqrt(HEAD)))
        parts.append(d_held)
    if wide > qkv_width:
        parts.append(jnp.zeros((2 * rows, wide - qkv_width), F32))
    d_packed = jnp.concatenate(parts, axis=1)
    d_packed = turn(d_packed, cos_ref[...], -upper_ref[...], -lower_ref[...]).astype(BF)
    d_packed_ref[...] = d_packed
    d_first = dot_last(d_packed, first_w_ref[:, :wide])
    xhat = xhat_ref[...]
    inner = d_first * vector_ref[0:1] + d_second * vector_ref[2:3]
    average = jnp.mean(inner, axis=-1, keepdims=True)
    along = jnp.mean(inner * xhat, axis=-1, keepdims=True)
    total = (inner - average - xhat * along) * scale_ref[:, 0:1]
    mine_ref[...] = total[:rows]
    other_ref[...] = total[rows:]

    def add_rows(block):
        return jnp.sum(block, axis=0, keepdims=True)

    width = sums_ref.shape[1]
    packed_sum = add_rows(d_packed.astype(F32))
    if wide < width:
        packed_sum = jnp.concatenate([packed_sum, jnp.zeros((1, width - wide), F32)], axis=1)
    sums_ref[...] = jnp.concatenate(
        [
            add_rows(d_first * xhat),
            add_rows(d_first),
            add_rows(d_second * xhat),
            add_rows(d_second),
            add_rows(grad.astype(F32)) * 0.25,
            add_rows(d_pre.astype(F32)),
            packed_sum,
            jnp.zeros((1, width), F32),
        ],
        axis=0,
    )


def weight_kernel(heads, depth, count, *refs):
    refs = list(refs)
    groups = [refs[i * 9 : (i + 1) * 9] for i in range(count)]
    first_out_ref, second_out_ref, full_refs = (
        refs[9 * count + count],
        refs[9 * count + count + 1],
        refs[9 * count : 9 * count + count],
    )
    qkv_width = heads * 3 * HEAD
    tile = first_out_ref.shape[0]

    def both(index):
        return jnp.concatenate([group[index][...] for group in groups], axis=0)

    def both_grads():
        parts = []
        for group in groups:
            parts += [group[2][...], group[3][...]]
        return jnp.concatenate(parts, axis=0)

    first, second, grad = both(0), both(1), both_grads()
    d_packed, d_pre, mixed, act = both(4), both(5), both(6), both(7)
    hidden = d_pre.shape[1]
    sums = sum(group[8][...] for group in groups[1:]) + groups[0][8][...]
    full = sum(item[...] for item in full_refs[1:]) + full_refs[0][...]
    long_row = jnp.concatenate([full[6:7, :qkv_width], full[5:6, :hidden]], axis=1)
    pieces = long_row.shape[1] // depth
    stacked = jnp.concatenate(
        [long_row[:, i * depth : (i + 1) * depth] for i in range(pieces)], axis=0
    )
    stacked = jnp.concatenate([stacked] * (tile // depth), axis=1)
    rest = SMALL - 8 - pieces
    small = jnp.concatenate([sums, stacked, jnp.zeros((rest, tile), F32)], axis=0)
    first_out_ref[...] = jnp.concatenate(
        [
            dot_first(first, d_packed)[:, :qkv_width],
            dot_first(grad, mixed),
            jnp.transpose(small),
        ],
        axis=1,
    ).astype(BF)
    second_out_ref[:, :hidden] = dot_first(second, d_pre).astype(BF)
    second_out_ref[:, hidden:] = dot_first(grad, act).astype(BF)


def cost(flops, moved):
    return pl.CostEstimate(flops=int(flops), bytes_accessed=int(moved), transcendentals=0)


def forward_call(own, far, weights, biases, layout, heads):
    rows, model = own.shape
    full = 2 * rows
    first_w, second_w = weights
    hidden = second_w.shape[1] // 2
    wide = layout[0].shape[1]

    def shape(height, width, kind):
        return jax.ShapeDtypeStruct((height, width), kind)

    outs = (
        shape(rows, model, F32),
        shape(rows, model, F32),
        shape(full, model, BF),
        shape(full, model, BF),
        shape(full, model, F32),
        shape(full, 128, F32),
        shape(full, wide, BF),
        shape(full, heads * HEAD, BF),
        shape(full, hidden, F32),
        shape(full, hidden, BF),
        shape(8, model, F32),
    )
    return pl.pallas_call(
        functools.partial(forward_kernel, heads),
        out_shape=outs,
        compiler_params=pltpu.CompilerParams(vmem_limit_bytes=VMEM_LIMIT),
        cost_estimate=cost(4e9, 8e6),
        name="forward",
    )(own, far, first_w, second_w, biases[0], biases[1], *layout)


def backward_call(own, far, weights, layout, kept, heads):
    rows, model = own.shape
    full = 2 * rows
    first_w, second_w = weights
    hidden = second_w.shape[1] // 2
    wide = layout[0].shape[1]
    norm1, norm2, xhat, scale, packed, mixed, pre, act, vectors = kept
    outs = (
        jax.ShapeDtypeStruct((rows, model), F32),
        jax.ShapeDtypeStruct((rows, model), F32),
        jax.ShapeDtypeStruct((full, wide), BF),
        jax.ShapeDtypeStruct((full, hidden), BF),
        jax.ShapeDtypeStruct((8, model), F32),
    )
    return pl.pallas_call(
        functools.partial(backward_kernel, heads),
        out_shape=outs,
        compiler_params=pltpu.CompilerParams(vmem_limit_bytes=VMEM_LIMIT),
        cost_estimate=cost(8e9, 10e6),
        name="backward",
    )(own, far, first_w, second_w, *layout, xhat, scale, packed, pre, vectors)


def weight_call(grads, kept, backs, heads, depth):
    model = kept[0][0].shape[1]
    hidden = kept[0][7].shape[1]
    tile = model // 2
    first_width = heads * 4 * HEAD + SMALL
    operands, specs = [], []

    def tiled(array):
        operands.append(array)
        specs.append(pl.BlockSpec((array.shape[0], tile), lambda i: (0, i)))

    def whole(array):
        operands.append(array)
        specs.append(pl.BlockSpec(array.shape, lambda i: (0, 0)))

    for (own, far), keep, back in zip(grads, kept, backs):
        tiled(keep[0])
        tiled(keep[1])
        tiled(own)
        tiled(far)
        whole(back[2])
        whole(back[3])
        whole(keep[5])
        whole(keep[7])
        tiled(back[4])
    for back in backs:
        whole(back[4])
    return pl.pallas_call(
        functools.partial(weight_kernel, heads, depth, len(grads)),
        grid=(2,),
        in_specs=specs,
        out_specs=(
            pl.BlockSpec((tile, first_width), lambda i: (i, 0)),
            pl.BlockSpec((tile, 2 * hidden), lambda i: (i, 0)),
        ),
        out_shape=(
            jax.ShapeDtypeStruct((model, first_width), BF),
            jax.ShapeDtypeStruct((model, 2 * hidden), BF),
        ),
        compiler_params=pltpu.CompilerParams(vmem_limit_bytes=VMEM_LIMIT),
        cost_estimate=cost(8e9, 10e6),
        name="weights",
    )(*operands)


def layout_of(lengths, rows, first_row, heads):
    full = 2 * rows
    ends = jnp.cumsum(lengths)
    places = (jnp.arange(full, dtype=jnp.int32) + first_row) % full
    segment = jnp.sum((places[:, None] >= ends[None, :]).astype(jnp.int32), axis=1)
    picked = segment[:, None] == jnp.arange(lengths.shape[0], dtype=jnp.int32)[None, :]
    position = places - jnp.sum(jnp.where(picked, (ends - lengths)[None, :], 0), axis=1)
    allowed = (segment[:, None] == segment[None, :]) & (places[:, None] >= places[None, :])
    bias = jnp.where(allowed, 0.0, NEG_BIG).astype(F32)
    half = ROT // 2
    inverse = jnp.exp(jnp.arange(half, dtype=F32) * (-2.0 * math.log(10000.0) / ROT))
    angles = position.astype(F32)[:, None] * inverse
    cosine, sine = jnp.cos(angles), jnp.sin(angles)
    plain = jnp.ones((full, HEAD - ROT), F32)
    empty = jnp.zeros((full, HEAD - ROT), F32)
    none = jnp.zeros((full, half), F32)
    cos_head = jnp.concatenate([cosine, cosine, plain], axis=1)
    upper_head = jnp.concatenate([-sine, none, empty], axis=1)
    lower_head = jnp.concatenate([none, sine, empty], axis=1)

    def spread(head, fill):
        rest = jnp.full((full, HEAD), fill, F32)
        table = jnp.concatenate([head, head, rest] * heads, axis=1)
        pad = -table.shape[1] % 128
        return jnp.concatenate([table, jnp.full((full, pad), fill, F32)], axis=1) if pad else table

    return spread(cos_head, 1.0), spread(upper_head, 0.0), spread(lower_head, 0.0), bias


def local(
    inputs,
    lengths,
    ln1_gain,
    ln1_shift,
    ln2_gain,
    ln2_shift,
    qkv_weight,
    qkv_bias,
    out_weight,
    fc_weight,
    fc_bias,
    proj_weight,
    branch_bias,
    cotangent,
):
    micro, rows, model = inputs.shape
    count = lax.axis_size("dp")
    pipe = lax.axis_index("pipe")
    core = lax.axis_index("tensor")
    leading = pipe == 0
    depth = qkv_weight.shape[1]
    qkv_width = qkv_weight.shape[2] // 2
    out_width = out_weight.shape[1] // 2
    hidden = fc_weight.shape[2] // 2
    heads = out_width // HEAD
    ahead_steps = count // 2

    vectors = jnp.concatenate([ln1_gain, ln1_shift, ln2_gain, ln2_shift, branch_bias], axis=0)
    vectors = jnp.pad(jnp.transpose(vectors), ((0, 0), (0, SMALL - 5)))
    out_turned = jnp.transpose(out_weight[0])
    proj_turned = jnp.transpose(proj_weight[0])

    def cut(array, width, index):
        return array[:, index * width : (index + 1) * width]

    def quarter(index):
        first = jnp.concatenate(
            [cut(qkv_weight[0], qkv_width, index), cut(out_turned, out_width, index), vectors],
            axis=1,
        )
        second = jnp.concatenate(
            [cut(fc_weight[0], hidden, index), cut(proj_turned, hidden, index)], axis=1
        )
        bias = jnp.concatenate([cut(qkv_bias, qkv_width, index), cut(fc_bias, hidden, index)], 1)
        return first, second, bias

    lower_part, upper_part = quarter(0), quarter(1)
    chunks = []
    for low_item, high_item in zip(lower_part, upper_part):
        kept_item = jnp.where(leading, low_item, high_item)
        sent_item = jnp.where(leading, high_item, low_item)
        came_item = swap(sent_item, "pipe")
        chunks.append(
            (
                jnp.where(leading, kept_item, came_item),
                jnp.where(leading, came_item, kept_item),
            )
        )
    weights, biases = [], []
    for section in range(2):
        weights.append(
            (
                ring_gather(chunks[0][section], ahead_steps),
                ring_gather(chunks[1][section], count - 1 - ahead_steps),
            )
        )
        long_bias = chunks[2][section].astype(F32)
        first_bias = long_bias[:, :qkv_width]
        pad = -qkv_width % 128
        biases.append((jnp.pad(first_bias, ((0, 0), (0, pad))), long_bias[:, qkv_width:]))

    layouts = [layout_of(lengths[m, 0], rows, core * rows, heads) for m in range(micro)]

    def complete(half, base):
        came = swap(half, "pipe")
        return (base + (half.astype(F32) + came.astype(F32))).astype(BF)

    def half_sum(mine, other):
        return (mine + swap(other, "tensor")).astype(BF)

    current = [(inputs[m], swap(inputs[m], "tensor")) for m in range(micro)]
    cotangents = [(cotangent[m], swap(cotangent[m], "tensor")) for m in range(micro)]
    stored, outputs = [], []
    for section in range(2):
        kept_rows, results = [], []
        for m in range(micro):
            own, far = current[m]
            found = forward_call(own, far, weights[section], biases[section], layouts[m], heads)
            kept_rows.append(found[2:])
            half = half_sum(found[0], found[1])
            base = own.astype(F32) + found[-1][4:5]
            results.append(complete(half, base))
        if section == 0:
            current = [(item, swap(item, "tensor")) for item in results]
        stored.append(kept_rows)
        outputs.append(results)

    grads = cotangents
    back_outputs, reduced = [None, None], [None, None]
    for section in (1, 0):
        backs, results = [], []
        for m in range(micro):
            own, far = grads[m]
            found = backward_call(
                own, far, weights[section], layouts[m], stored[section][m], heads
            )
            backs.append(found)
            half = half_sum(found[0], found[1])
            results.append(complete(half, own.astype(F32)))
        first_terms, second_terms = weight_call(grads, stored[section], backs, heads, depth)
        reduced[section] = (
            ring_scatter(first_terms, ahead_steps),
            ring_scatter(second_terms, count - 1 - ahead_steps),
        )
        back_outputs[section] = results
        if section == 1:
            grads = [(item, swap(item, "tensor")) for item in results]

    activations = jnp.where(leading, jnp.stack(outputs[0]), jnp.stack(outputs[1]))[None]
    input_grads = jnp.where(leading, jnp.stack(back_outputs[0]), jnp.stack(back_outputs[1]))[None]

    halves = []
    for index in range(2):
        own = jnp.where(leading, reduced[0][index], reduced[1][index])
        given = jnp.where(leading, reduced[1][index], reduced[0][index]).astype(BF)
        came = swap(given, "pipe").astype(F32)
        halves.append((own, came))

    def joined(index, start, width):
        own, came = (item[:, start : start + width] for item in halves[index])
        lower_item = jnp.where(leading, own, came)
        upper_item = jnp.where(leading, came, own)
        return jnp.concatenate([lower_item, upper_item], axis=1)

    small_start = qkv_width + out_width
    own_small, came_small = (item[:, small_start:] for item in halves[0])
    vector_grads = own_small[:, :8] + came_small[:, :8]
    vector_grads = jnp.transpose(vector_grads + swap(vector_grads, "tensor"))
    pieces = (qkv_width + hidden) // depth

    def flat(block):
        return jnp.transpose(block[:, 8 : 8 + pieces]).reshape(1, -1)

    own_bias, came_bias = flat(own_small), flat(came_small)
    lower_bias = jnp.where(leading, own_bias, came_bias)
    upper_bias = jnp.where(leading, came_bias, own_bias)
    qkv_bias_grad = jnp.concatenate([lower_bias[:, :qkv_width], upper_bias[:, :qkv_width]], axis=1)
    fc_bias_grad = jnp.concatenate([lower_bias[:, qkv_width:], upper_bias[:, qkv_width:]], axis=1)
    return (
        activations,
        input_grads,
        vector_grads[0:1],
        vector_grads[1:2],
        vector_grads[2:3],
        vector_grads[3:4],
        joined(0, 0, qkv_width)[None],
        qkv_bias_grad,
        jnp.transpose(joined(0, qkv_width, out_width))[None],
        joined(1, 0, hidden)[None],
        fc_bias_grad,
        jnp.transpose(joined(1, hidden, hidden))[None],
        vector_grads[4:5],
    )


def solution(mesh):
    rows = P(None, ("dp", "tensor"), None)
    vector = P("pipe", "dp")
    bias = P("pipe", "tensor")
    wide = P("pipe", "dp", "tensor")
    tall = P("pipe", "tensor", "dp")
    result = P("pipe", None, ("dp", "tensor"), None)
    return jax.shard_map(
        local,
        mesh=mesh,
        in_specs=(
            rows,
            P(None, "dp", None),
            vector,
            vector,
            vector,
            vector,
            wide,
            bias,
            tall,
            wide,
            bias,
            tall,
            vector,
            rows,
        ),
        out_specs=(
            result,
            result,
            vector,
            vector,
            vector,
            vector,
            wide,
            bias,
            tall,
            wide,
            bias,
            tall,
            vector,
        ),
        check_vma=False,
    )
```

```python
import functools
import math

import jax
import jax.numpy as jnp
from jax import lax
from jax.experimental import pallas as pl
from jax.experimental.pallas import tpu as pltpu
from jax.sharding import PartitionSpec as P

HEAD = 64
ROT = 16
EPSILON = 1e-05
NEG_BIG = -1e30
VMEM_LIMIT = 16 * 1024 * 1024
BF = jnp.bfloat16
F32 = jnp.float32
SMALL = 128
TIES = 2


def ring_device(place, count):
    if count == 8:
        return jnp.where(place < 4, 2 * place, 15 - 2 * place)
    if count == 32:
        folded = jnp.where(place < 16, place, 31 - place)
        row, column = folded // 4, folded % 4
        column = jnp.where(row % 2 == 0, column, 3 - column)
        return row * 4 + column + jnp.where(place < 16, 0, 16)
    return place


def ring_place(device, count):
    if count == 8:
        half = device // 2
        return jnp.where(device % 2 == 0, half, 7 - half)
    if count == 32:
        within = device % 16
        row, column = within // 4, within % 4
        column = jnp.where(row % 2 == 0, column, 3 - column)
        folded = row * 4 + column
        return jnp.where(device < 16, folded, 31 - folded)
    return device


def ring_list(count):
    if count == 8:
        return [0, 2, 4, 6, 7, 5, 3, 1]
    if count == 32:
        snake = []
        for row in range(4):
            line = [row * 4 + column for column in range(4)]
            snake += line if row % 2 == 0 else line[::-1]
        return snake + [16 + item for item in reversed(snake)]
    return list(range(count))


def ring_routes(count):
    order = ring_list(count)
    ahead = [(order[i], order[(i + 1) % count]) for i in range(count)]
    return ahead, [(target, source) for source, target in ahead]


def after(value, *earlier):
    return lax.optimization_barrier((value, *earlier))[0]


def tie(values, earlier):
    present = [item for item in values if item is not None]
    if not earlier or not present:
        return values
    tied = list(lax.optimization_barrier((*present, *earlier))[: len(present)])
    return [None if item is None else tied.pop(0) for item in values]


class RingGather:
    def __init__(self, chunk, whole, forward_steps):
        self.count = lax.axis_size("dp")
        self.ahead, self.behind = ring_routes(self.count)
        self.place = ring_place(lax.axis_index("dp"), self.count)
        self.depth = chunk.shape[0]
        self.limits = (forward_steps, self.count - 1 - forward_steps)
        self.steps = max(self.limits)
        self.step = 0
        self.front = self.back = chunk
        self.whole = lax.dynamic_update_slice(
            whole, chunk, (lax.axis_index("dp") * self.depth, 0)
        )

    def put(self, block, distance):
        owner = ring_device((self.place + self.count + distance) % self.count, self.count)
        self.whole = lax.dynamic_update_slice(self.whole, block, (owner * self.depth, 0))

    def advance(self, *earlier):
        self.step += 1
        front = self.front if self.step <= self.limits[0] else None
        back = self.back if self.step <= self.limits[1] else None
        front, back = tie([front, back], earlier)
        if front is not None:
            self.front = lax.ppermute(front, "dp", self.ahead)
            self.put(self.front, -self.step)
        if back is not None:
            self.back = lax.ppermute(back, "dp", self.behind)
            self.put(self.back, self.step)
        return [item for item in (front, back) if item is not None]

    def result(self):
        while self.step < self.steps:
            self.advance()
        return self.whole


class RingScatter:
    def __init__(self, terms, forward_steps):
        self.terms = terms
        self.count = lax.axis_size("dp")
        self.place = ring_place(lax.axis_index("dp"), self.count)
        self.depth = terms.shape[0] // self.count
        self.ahead, self.behind = ring_routes(self.count)
        self.forward_steps = forward_steps
        self.backward_steps = self.count - 1 - forward_steps
        self.steps = max(self.forward_steps, self.backward_steps)
        self.step = 0
        self.front = self.back = None

    def term(self, distance):
        owner = ring_device((self.place + self.count + distance) % self.count, self.count)
        width = self.terms.shape[1]
        return lax.dynamic_slice(self.terms, (owner * self.depth, 0), (self.depth, width))

    def advance(self, *earlier):
        marks = []
        front, back = tie([self.front, self.back], earlier)
        if self.step < self.forward_steps:
            own = self.term(self.forward_steps - self.step)
            if front is not None:
                own = (own.astype(F32) + front.astype(F32)).astype(BF)
            marks.append(own)
            front = lax.ppermute(own, "dp", self.ahead)
        if self.step < self.backward_steps:
            own = self.term(self.step - self.backward_steps)
            if back is not None:
                own = (own.astype(F32) + back.astype(F32)).astype(BF)
            marks.append(own)
            back = lax.ppermute(own, "dp", self.behind)
        self.front, self.back = front, back
        self.step += 1
        return marks

    def result(self):
        while self.step < self.steps:
            self.advance()
        return self.term(0).astype(F32) + self.front.astype(F32) + self.back.astype(F32)


def swap(block, axis):
    return lax.ppermute(block, axis, [(0, 1), (1, 0)])


def dot(left, right):
    return jnp.dot(left, right, preferred_element_type=F32)


def dot_last(left, right):
    return lax.dot_general(left, right, (((1,), (1,)), ((), ())), preferred_element_type=F32)


def dot_first(left, right):
    return lax.dot_general(left, right, (((0,), (0,)), ((), ())), preferred_element_type=F32)


def softmax_rows(queries, keys, bias):
    scores = dot_last(queries, keys) * (1.0 / math.sqrt(HEAD)) + bias
    peak = jnp.max(scores, axis=-1, keepdims=True)
    expons = jnp.exp(scores - peak)
    return expons / jnp.sum(expons, axis=-1, keepdims=True)


def head_parts(packed, index):
    base = index * 3 * HEAD
    return tuple(packed[:, base + j * HEAD : base + (j + 1) * HEAD] for j in range(3))


def turn(values, cosine, upper, lower):
    width = values.shape[1]
    return (
        values * cosine
        + pltpu.roll(values, width - ROT // 2, 1) * upper
        + pltpu.roll(values, ROT // 2, 1) * lower
    )


def pack_kernel(pipe_ref, *refs):
    sources, (kept_ref, sent_ref) = refs[:6], refs[6:8]
    held, marks = refs[10:16], refs[16]
    copies = [
        pltpu.make_async_copy(source, target, marks.at[i])
        for i, (source, target) in enumerate(zip(sources, held))
    ]
    for copy in copies:
        copy.start()
    for copy in copies:
        copy.wait()
    qkv_ref, out_ref, fc_ref, proj_ref = held[:4]
    depth = qkv_ref.shape[0]
    rows = [held[4][...]]
    long_bias = held[5][...]
    qkv_width, out_width = qkv_ref.shape[1] // 2, out_ref.shape[1] // 2
    hidden = fc_ref.shape[1] // 2
    start = qkv_width + out_width
    qkv_bias, fc_bias = long_bias[:, : 2 * qkv_width], long_bias[:, 2 * qkv_width :]

    def fill(target, index):
        target[:, :start] = jnp.concatenate(
            [
                qkv_ref[:, index * qkv_width : (index + 1) * qkv_width],
                out_ref[:, index * out_width : (index + 1) * out_width],
            ],
            axis=1,
        )
        target[:, start : start + hidden] = fc_ref[:, index * hidden : (index + 1) * hidden]
        target[:, start + hidden : start + 2 * hidden] = proj_ref[
            :, index * hidden : (index + 1) * hidden
        ]
        bias = jnp.concatenate(
            [
                qkv_bias[:, index * qkv_width : (index + 1) * qkv_width],
                fc_bias[:, index * hidden : (index + 1) * hidden],
            ],
            axis=1,
        )
        pieces = bias.shape[1] // depth
        small = rows + [bias[:, i * depth : (i + 1) * depth] for i in range(pieces)]
        small.append(jnp.zeros((SMALL - 8 - pieces, depth), F32))
        small = jnp.transpose(jnp.concatenate(small, axis=0))
        target[:, start + 2 * hidden :] = small.astype(BF)

    @pl.when(pipe_ref[0] == 0)
    def _():
        fill(kept_ref, 0)
        fill(sent_ref, 1)

    @pl.when(pipe_ref[0] != 0)
    def _():
        fill(kept_ref, 1)
        fill(sent_ref, 0)


def forward_kernel(
    heads,
    depth,
    own_ref,
    far_ref,
    weight_ref,
    cos_ref,
    upper_ref,
    lower_ref,
    bias_ref,
    mine_ref,
    other_ref,
    norm1_ref,
    norm2_ref,
    xhat_ref,
    scale_ref,
    packed_ref,
    mixed_ref,
    pre_ref,
    act_ref,
    vector_ref,
):
    rows = own_ref.shape[0]
    qkv_width = heads * 3 * HEAD
    start = heads * 4 * HEAD
    wide = cos_ref.shape[1]
    hidden = pre_ref.shape[1]
    pieces = (qkv_width + hidden) // depth
    small = jnp.transpose(weight_ref[:, start + 2 * hidden :].astype(F32))
    vectors = small[:8]
    vector_ref[...] = vectors
    long_bias = jnp.concatenate([small[8 + i : 9 + i, :depth] for i in range(pieces)], axis=1)
    qkv_bias = jnp.concatenate(
        [long_bias[:, :qkv_width], jnp.zeros((1, wide - qkv_width), F32)], axis=1
    )
    fc_bias = long_bias[:, qkv_width:]
    values = jnp.concatenate([own_ref[...], far_ref[...]], axis=0).astype(F32)
    centred = values - jnp.mean(values, axis=-1, keepdims=True)
    scale = lax.rsqrt(jnp.mean(centred * centred, axis=-1, keepdims=True) + EPSILON)
    xhat = centred * scale
    xhat_ref[...] = xhat
    scale_ref[...] = jnp.broadcast_to(scale, scale_ref.shape)
    first = (xhat * vectors[0:1] + vectors[1:2]).astype(BF)
    second = (xhat * vectors[2:3] + vectors[3:4]).astype(BF)
    norm1_ref[...] = first
    norm2_ref[...] = second
    packed = dot(first, weight_ref[:, :wide]) + qkv_bias
    packed = turn(packed, cos_ref[...], upper_ref[...], lower_ref[...]).astype(BF)
    packed_ref[...] = packed
    bias = bias_ref[...]
    mixed = []
    for index in range(heads):
        queries, keys, held = head_parts(packed, index)
        weights = softmax_rows(queries, keys, bias).astype(BF)
        mixed.append(dot(weights, held))
    mixed = jnp.concatenate(mixed, axis=1).astype(BF)
    mixed_ref[...] = mixed
    pre = dot(second, weight_ref[:, start : start + hidden]) + fc_bias
    pre_ref[...] = pre
    act = (pre * (0.5 + 0.5 * lax.erf(pre * math.sqrt(0.5)))).astype(BF)
    act_ref[...] = act
    total = dot_last(act, weight_ref[:, start + hidden : start + 2 * hidden])
    total = total + dot_last(mixed, weight_ref[:, qkv_width:start])
    mine_ref[...] = total[:rows]
    other_ref[...] = total[rows:]


def backward_kernel(
    heads,
    own_ref,
    far_ref,
    weight_ref,
    cos_ref,
    upper_ref,
    lower_ref,
    bias_ref,
    xhat_ref,
    scale_ref,
    packed_ref,
    pre_ref,
    vector_ref,
    mine_ref,
    other_ref,
    d_packed_ref,
    d_pre_ref,
    sums_ref,
):
    rows = own_ref.shape[0]
    qkv_width = heads * 3 * HEAD
    start = heads * 4 * HEAD
    wide = cos_ref.shape[1]
    hidden = pre_ref.shape[1]
    grad = jnp.concatenate([own_ref[...], far_ref[...]], axis=0)
    d_act = dot(grad, weight_ref[:, start + hidden : start + 2 * hidden])
    pre = pre_ref[...]
    slope = 0.5 + 0.5 * lax.erf(pre * math.sqrt(0.5))
    slope = slope + pre * (jnp.exp(pre * pre * -0.5) * (1.0 / math.sqrt(2.0 * math.pi)))
    d_pre = (d_act * slope).astype(BF)
    d_pre_ref[...] = d_pre
    d_second = dot_last(d_pre, weight_ref[:, start : start + hidden])
    d_mixed = dot(grad, weight_ref[:, qkv_width:start]).astype(BF)
    bias = bias_ref[...]
    packed = packed_ref[...]
    parts = []
    for index in range(heads):
        queries, keys, held = head_parts(packed, index)
        weights = softmax_rows(queries, keys, bias)
        given = d_mixed[:, index * HEAD : (index + 1) * HEAD]
        d_held = dot_first(weights.astype(BF), given)
        d_weights = dot_last(given, held)
        row_dot = jnp.sum(weights * d_weights, axis=-1, keepdims=True)
        d_scores = (weights * (d_weights - row_dot)).astype(BF)
        parts.append(dot(d_scores, keys) * (1.0 / math.sqrt(HEAD)))
        parts.append(dot_first(d_scores, queries) * (1.0 / math.sqrt(HEAD)))
        parts.append(d_held)
    if wide > qkv_width:
        parts.append(jnp.zeros((2 * rows, wide - qkv_width), F32))
    d_packed = jnp.concatenate(parts, axis=1)
    d_packed = turn(d_packed, cos_ref[...], -upper_ref[...], -lower_ref[...]).astype(BF)
    d_packed_ref[...] = d_packed
    d_first = dot_last(d_packed, weight_ref[:, :wide])
    xhat = xhat_ref[...]
    inner = d_first * vector_ref[0:1] + d_second * vector_ref[2:3]
    average = jnp.mean(inner, axis=-1, keepdims=True)
    along = jnp.mean(inner * xhat, axis=-1, keepdims=True)
    total = (inner - average - xhat * along) * scale_ref[:, 0:1]
    mine_ref[...] = total[:rows]
    other_ref[...] = total[rows:]

    def add_rows(block):
        return jnp.sum(block, axis=0, keepdims=True)

    width = sums_ref.shape[1]
    packed_sum = add_rows(d_packed.astype(F32))
    if wide < width:
        packed_sum = jnp.concatenate([packed_sum, jnp.zeros((1, width - wide), F32)], axis=1)
    sums_ref[...] = jnp.concatenate(
        [
            add_rows(d_first * xhat),
            add_rows(d_first),
            add_rows(d_second * xhat),
            add_rows(d_second),
            add_rows(grad.astype(F32)) * 0.25,
            add_rows(d_pre.astype(F32)),
            packed_sum,
            jnp.zeros((1, width), F32),
        ],
        axis=0,
    )


def weight_kernel(heads, depth, count, *refs):
    refs = list(refs)
    groups = [refs[i * 9 : (i + 1) * 9] for i in range(count)]
    terms_ref, full_refs = refs[10 * count], refs[9 * count : 10 * count]
    qkv_width = heads * 3 * HEAD
    start = heads * 4 * HEAD
    tile = terms_ref.shape[0]

    def both(index):
        return jnp.concatenate([group[index][...] for group in groups], axis=0)

    def both_grads():
        parts = []
        for group in groups:
            parts += [group[2][...], group[3][...]]
        return jnp.concatenate(parts, axis=0)

    first, second, grad = both(0), both(1), both_grads()
    d_packed, d_pre, mixed, act = both(4), both(5), both(6), both(7)
    hidden = d_pre.shape[1]
    sums = sum(group[8][...] for group in groups[1:]) + groups[0][8][...]
    full = sum(item[...] for item in full_refs[1:]) + full_refs[0][...]
    long_row = jnp.concatenate([full[6:7, :qkv_width], full[5:6, :hidden]], axis=1)
    pieces = long_row.shape[1] // depth
    stacked = jnp.concatenate(
        [long_row[:, i * depth : (i + 1) * depth] for i in range(pieces)], axis=0
    )
    stacked = jnp.concatenate([stacked] * (tile // depth), axis=1)
    rest = SMALL - 8 - pieces
    small = jnp.concatenate([sums, stacked, jnp.zeros((rest, tile), F32)], axis=0)
    terms_ref[:, :start] = jnp.concatenate(
        [dot_first(first, d_packed)[:, :qkv_width], dot_first(grad, mixed)], axis=1
    ).astype(BF)
    terms_ref[:, start : start + hidden] = dot_first(second, d_pre).astype(BF)
    terms_ref[:, start + hidden : start + 2 * hidden] = dot_first(grad, act).astype(BF)
    terms_ref[:, start + 2 * hidden :] = jnp.transpose(small).astype(BF)


def unpack_kernel(
    pipe_ref,
    own_ref,
    came_ref,
    own_small_ref,
    came_small_ref,
    qkv_ref,
    qkv_bias_ref,
    out_ref,
    fc_ref,
    fc_bias_ref,
    proj_ref,
    *vector_refs,
):
    depth = qkv_ref.shape[0]
    qkv_width, out_width = qkv_ref.shape[1] // 2, out_ref.shape[1] // 2
    hidden = fc_ref.shape[1] // 2
    start = qkv_width + out_width
    pieces = (qkv_width + hidden) // depth
    smalls = [jnp.transpose(ref[...]) for ref in (own_small_ref, came_small_ref)]
    vectors = smalls[0][:8] + smalls[1][:8]
    for index, ref in enumerate(vector_refs):
        ref[...] = vectors[index : index + 1]
    longs = [
        jnp.concatenate([small[8 + i : 9 + i] for i in range(pieces)], axis=1) for small in smalls
    ]

    def fill(lower, upper, low_bias, high_bias):
        for index, (block, bias) in enumerate(((lower, low_bias), (upper, high_bias))):
            columns = slice(index * qkv_width, (index + 1) * qkv_width)
            qkv_ref[:, columns] = block[:, :qkv_width].astype(F32)
            qkv_bias_ref[:, columns] = bias[:, :qkv_width]
            lines = slice(index * out_width, (index + 1) * out_width)
            out_ref[:, lines] = block[:, qkv_width:start].astype(F32)
            units = slice(index * hidden, (index + 1) * hidden)
            fc_ref[:, units] = block[:, start : start + hidden].astype(F32)
            fc_bias_ref[:, units] = bias[:, qkv_width:]
            proj_ref[:, units] = block[:, start + hidden : start + 2 * hidden].astype(F32)

    @pl.when(pipe_ref[0] == 0)
    def _():
        fill(own_ref, came_ref, longs[0], longs[1])

    @pl.when(pipe_ref[0] != 0)
    def _():
        fill(came_ref, own_ref, longs[1], longs[0])


def cost(flops, moved):
    return pl.CostEstimate(flops=int(flops), bytes_accessed=int(moved), transcendentals=0)


def in_vmem():
    return pl.BlockSpec(memory_space=pltpu.VMEM)


def pack_call(pipe, arrays, count):
    qkv, out, fc = arrays[:3]
    width = (qkv.shape[1] + out.shape[1]) // 2 + fc.shape[1] + SMALL
    packet = jax.ShapeDtypeStruct((qkv.shape[0], width), BF)
    whole = jax.ShapeDtypeStruct((count * qkv.shape[0], width), BF)
    return pl.pallas_call(
        pack_kernel,
        out_shape=(packet, packet, whole, whole),
        out_specs=(in_vmem(), in_vmem())
        + (pl.BlockSpec(memory_space=pl.ANY), pl.BlockSpec(memory_space=pl.ANY)),
        in_specs=[pl.BlockSpec(memory_space=pltpu.SMEM)]
        + [pl.BlockSpec(memory_space=pl.ANY)] * len(arrays),
        scratch_shapes=[pltpu.VMEM(item.shape, item.dtype) for item in arrays]
        + [pltpu.SemaphoreType.DMA((len(arrays),))],
        compiler_params=pltpu.CompilerParams(vmem_limit_bytes=VMEM_LIMIT),
        cost_estimate=cost(0, 4e6),
        name="pack",
    )(pipe, *arrays)


def unpack_call(pipe, own, came, own_small, came_small, widths):
    depth = own.shape[0]
    qkv_width, out_width, hidden = widths
    shapes = (
        (depth, 2 * qkv_width),
        (1, 2 * qkv_width),
        (depth, 2 * out_width),
        (depth, 2 * hidden),
        (1, 2 * hidden),
        (depth, 2 * hidden),
    ) + ((1, depth),) * 5
    return pl.pallas_call(
        unpack_kernel,
        out_shape=tuple(jax.ShapeDtypeStruct(shape, F32) for shape in shapes),
        in_specs=[pl.BlockSpec(memory_space=pltpu.SMEM)] + [in_vmem()] * 4,
        compiler_params=pltpu.CompilerParams(vmem_limit_bytes=VMEM_LIMIT),
        cost_estimate=cost(0, 6e6),
        name="unpack",
    )(pipe, own, came, own_small, came_small)


def forward_call(own, far, weight, layout, heads, hidden, depth):
    rows, model = own.shape
    full = 2 * rows
    wide = layout[0].shape[1]

    def shape(height, width, kind):
        return jax.ShapeDtypeStruct((height, width), kind)

    outs = (
        shape(rows, model, F32),
        shape(rows, model, F32),
        shape(full, model, BF),
        shape(full, model, BF),
        shape(full, model, F32),
        shape(full, 128, F32),
        shape(full, wide, BF),
        shape(full, heads * HEAD, BF),
        shape(full, hidden, F32),
        shape(full, hidden, BF),
        shape(8, model, F32),
    )
    return pl.pallas_call(
        functools.partial(forward_kernel, heads, depth),
        out_shape=outs,
        compiler_params=pltpu.CompilerParams(vmem_limit_bytes=VMEM_LIMIT),
        cost_estimate=cost(4e9, 8e6),
        name="forward",
    )(own, far, weight, *layout)


def backward_call(own, far, weight, layout, kept, heads):
    rows, model = own.shape
    full = 2 * rows
    wide = layout[0].shape[1]
    norm1, norm2, xhat, scale, packed, mixed, pre, act, vectors = kept
    outs = (
        jax.ShapeDtypeStruct((rows, model), F32),
        jax.ShapeDtypeStruct((rows, model), F32),
        jax.ShapeDtypeStruct((full, wide), BF),
        jax.ShapeDtypeStruct((full, pre.shape[1]), BF),
        jax.ShapeDtypeStruct((8, model), F32),
    )
    return pl.pallas_call(
        functools.partial(backward_kernel, heads),
        out_shape=outs,
        compiler_params=pltpu.CompilerParams(vmem_limit_bytes=VMEM_LIMIT),
        cost_estimate=cost(5e9, 10e6),
        name="backward",
    )(own, far, weight, *layout, xhat, scale, packed, pre, vectors)


def weight_call(grads, kept, backs, heads, depth):
    model = kept[0][0].shape[1]
    hidden = kept[0][7].shape[1]
    tile = model // 2
    width = heads * 4 * HEAD + 2 * hidden + SMALL
    operands, specs = [], []

    def tiled(array):
        operands.append(array)
        specs.append(pl.BlockSpec((array.shape[0], tile), lambda i: (0, i)))

    def whole(array):
        operands.append(array)
        specs.append(pl.BlockSpec(array.shape, lambda i: (0, 0)))

    for (own, far), keep, back in zip(grads, kept, backs):
        tiled(keep[0])
        tiled(keep[1])
        tiled(own)
        tiled(far)
        whole(back[2])
        whole(back[3])
        whole(keep[5])
        whole(keep[7])
        tiled(back[4])
    for back in backs:
        whole(back[4])
    return pl.pallas_call(
        functools.partial(weight_kernel, heads, depth, len(grads)),
        grid=(2,),
        in_specs=specs,
        out_specs=pl.BlockSpec((tile, width), lambda i: (i, 0)),
        out_shape=jax.ShapeDtypeStruct((model, width), BF),
        compiler_params=pltpu.CompilerParams(vmem_limit_bytes=VMEM_LIMIT),
        cost_estimate=cost(8e9, 10e6),
        name="weights",
    )(*operands)


def layout_of(lengths, rows, first_row, heads):
    full = 2 * rows
    ends = jnp.cumsum(lengths)
    places = (jnp.arange(full, dtype=jnp.int32) + first_row) % full
    segment = jnp.sum((places[:, None] >= ends[None, :]).astype(jnp.int32), axis=1)
    picked = segment[:, None] == jnp.arange(lengths.shape[0], dtype=jnp.int32)[None, :]
    position = places - jnp.sum(jnp.where(picked, (ends - lengths)[None, :], 0), axis=1)
    allowed = (segment[:, None] == segment[None, :]) & (places[:, None] >= places[None, :])
    bias = jnp.where(allowed, 0.0, NEG_BIG).astype(F32)
    half = ROT // 2
    inverse = jnp.exp(jnp.arange(half, dtype=F32) * (-2.0 * math.log(10000.0) / ROT))
    angles = position.astype(F32)[:, None] * inverse
    cosine, sine = jnp.cos(angles), jnp.sin(angles)
    plain = jnp.ones((full, HEAD - ROT), F32)
    empty = jnp.zeros((full, HEAD - ROT), F32)
    none = jnp.zeros((full, half), F32)
    cos_head = jnp.concatenate([cosine, cosine, plain], axis=1)
    upper_head = jnp.concatenate([-sine, none, empty], axis=1)
    lower_head = jnp.concatenate([none, sine, empty], axis=1)

    def spread(head, fill):
        rest = jnp.full((full, HEAD), fill, F32)
        table = jnp.concatenate([head, head, rest] * heads, axis=1)
        pad = -table.shape[1] % 128
        return jnp.concatenate([table, jnp.full((full, pad), fill, F32)], axis=1) if pad else table

    return spread(cos_head, 1.0), spread(upper_head, 0.0), spread(lower_head, 0.0), bias


def local(
    inputs,
    lengths,
    ln1_gain,
    ln1_shift,
    ln2_gain,
    ln2_shift,
    qkv_weight,
    qkv_bias,
    out_weight,
    fc_weight,
    fc_bias,
    proj_weight,
    branch_bias,
    cotangent,
):
    micro, rows, model = inputs.shape
    count = lax.axis_size("dp")
    pipe = lax.axis_index("pipe")
    core = lax.axis_index("tensor")
    leading = pipe == 0
    depth = qkv_weight.shape[1]
    qkv_width = qkv_weight.shape[2] // 2
    out_width = out_weight.shape[1] // 2
    hidden = fc_weight.shape[2] // 2
    heads = out_width // HEAD
    ahead_steps = count // 2

    pipe_word = pipe.astype(jnp.int32).reshape(1)
    vectors = jnp.concatenate([ln1_gain, ln1_shift, ln2_gain, ln2_shift, branch_bias], axis=0)
    vectors = jnp.pad(vectors.astype(F32), ((0, 3), (0, 0)))
    kept_part, sent_part, first_whole, second_whole = pack_call(
        pipe_word,
        (
            qkv_weight[0],
            jnp.transpose(out_weight[0]),
            fc_weight[0],
            jnp.transpose(proj_weight[0]),
            vectors,
            jnp.concatenate([qkv_bias, fc_bias], axis=1).astype(F32),
        ),
        count,
    )
    came_part = swap(sent_part, "pipe")
    chunk = jnp.where(leading, kept_part, came_part)
    gather = RingGather(chunk, first_whole, ahead_steps)
    gather.advance()
    later = RingGather(
        jnp.where(leading, came_part, kept_part), second_whole, count - 1 - ahead_steps
    )
    order = []
    for _ in range(gather.steps - 1):
        order = gather.advance(*order)
        if later.step < later.steps - 1:
            order = later.advance(*order)
    weights = [gather.result(), None]

    lengths = after(lengths, chunk)
    inputs, cotangent = after(inputs, sent_part), after(cotangent, chunk)
    layouts = [layout_of(lengths[m, 0], rows, core * rows, heads) for m in range(micro)]

    def complete(half, base):
        came = swap(half, "pipe")
        return (base + (half.astype(F32) + came.astype(F32))).astype(BF)

    def half_sum(mine, other):
        return (mine + swap(other, "tensor")).astype(BF)

    current = [(inputs[m], swap(inputs[m], "tensor")) for m in range(micro)]
    cotangents = [(cotangent[m], swap(cotangent[m], "tensor")) for m in range(micro)]
    stored, outputs = [], []
    for section in range(2):
        kept_rows, results = [], []
        for m in range(micro):
            own, far = current[m]
            found = forward_call(own, far, weights[section], layouts[m], heads, hidden, depth)
            kept_rows.append(found[2:])
            if section == 0 and m + 1 == micro:
                later.advance(found[-1])
                weights[1] = later.result()
            half = half_sum(found[0], found[1])
            base = own.astype(F32) + found[-1][4:5]
            results.append(complete(half, base))
        if section == 0:
            current = [(item, swap(item, "tensor")) for item in results]
        stored.append(kept_rows)
        outputs.append(results)

    back_outputs = [None, None]
    backs, results, halves = [], [], []
    for m in range(micro):
        own, far = cotangents[m]
        found = backward_call(own, far, weights[1], layouts[m], stored[1][m], heads)
        backs.append(found)
        halves.append(half_sum(found[0], found[1]))
        results.append(complete(halves[m], own.astype(F32)))
    back_outputs[1] = results
    grads = [(item, swap(item, "tensor")) for item in results]
    backs[-1] = (*backs[-1][:4], after(backs[-1][4], halves[-1]))
    scatter = RingScatter(weight_call(cotangents, stored[1], backs, heads, depth), ahead_steps)
    scatter.advance()
    backs, results, marks = [], [], ()
    for m in range(micro):
        own, far = grads[m]
        found = backward_call(own, far, weights[0], layouts[m], stored[0][m], heads)
        backs.append(found)
        results.append(complete(half_sum(found[0], found[1]), own.astype(F32)))
        if m + 1 < micro:
            marks = scatter.advance(found[4])
    back_outputs[0] = results
    backs[-1] = (*backs[-1][:4], after(backs[-1][4], *marks[:TIES]))
    terms = weight_call(grads, stored[0], backs, heads, depth)
    last = RingScatter(terms, count - 1 - ahead_steps)
    order = last.advance()
    while scatter.step < scatter.steps or last.step < last.steps:
        if scatter.step < scatter.steps:
            order = scatter.advance(*order[:TIES])
        if last.step < last.steps:
            order = last.advance(*order[:TIES])
    reduced = [last.result(), scatter.result()]

    activations = jnp.where(leading, jnp.stack(outputs[0]), jnp.stack(outputs[1]))[None]
    input_grads = jnp.where(leading, jnp.stack(back_outputs[0]), jnp.stack(back_outputs[1]))[None]

    start = qkv_width + out_width
    own_part = jnp.where(leading, reduced[0], reduced[1])
    given_part = jnp.where(leading, reduced[1], reduced[0])
    came_part = swap(given_part[:, : start + 2 * hidden].astype(BF), "pipe")
    smalls = jnp.concatenate(
        [own_part[:, start + 2 * hidden :], given_part[:, start + 2 * hidden :]], axis=0
    )
    lane = lax.broadcasted_iota(jnp.int32, smalls.shape, 1)
    smalls = jnp.where(lane < 8, smalls + swap(smalls, "tensor"), smalls)
    came_small = swap(smalls[depth:], "pipe")
    grads_out = unpack_call(
        pipe_word, own_part, came_part, smalls[:depth], came_small, (qkv_width, out_width, hidden)
    )
    qkv_grad, qkv_bias_grad, out_grad, fc_grad, fc_bias_grad, proj_grad = grads_out[:6]
    vector_grads = grads_out[6:]
    return (
        activations,
        input_grads,
        vector_grads[0],
        vector_grads[1],
        vector_grads[2],
        vector_grads[3],
        qkv_grad[None],
        qkv_bias_grad,
        jnp.transpose(out_grad)[None],
        fc_grad[None],
        fc_bias_grad,
        jnp.transpose(proj_grad)[None],
        vector_grads[4],
    )


def solution(mesh):
    rows = P(None, ("dp", "tensor"), None)
    vector = P("pipe", "dp")
    bias = P("pipe", "tensor")
    wide = P("pipe", "dp", "tensor")
    tall = P("pipe", "tensor", "dp")
    result = P("pipe", None, ("dp", "tensor"), None)
    return jax.shard_map(
        local,
        mesh=mesh,
        in_specs=(
            rows,
            P(None, "dp", None),
            vector,
            vector,
            vector,
            vector,
            wide,
            bias,
            tall,
            wide,
            bias,
            tall,
            vector,
            rows,
        ),
        out_specs=(
            result,
            result,
            vector,
            vector,
            vector,
            vector,
            wide,
            bias,
            tall,
            wide,
            bias,
            tall,
            vector,
        ),
        check_vma=False,
    )
```

```python
import functools
import math

import jax
import jax.numpy as jnp
from jax import lax
from jax.experimental import pallas as pl
from jax.experimental.pallas import tpu as pltpu
from jax.sharding import PartitionSpec as P

HEAD = 64
ROT = 16
EPSILON = 1e-05
NEG_BIG = -1e30
VMEM_LIMIT = 16 * 1024 * 1024
BF = jnp.bfloat16
F32 = jnp.float32
SMALL = 128
TIES = 2


def ring_device(place, count):
    if count == 8:
        return jnp.where(place < 4, 2 * place, 15 - 2 * place)
    if count == 32:
        folded = jnp.where(place < 16, place, 31 - place)
        row, column = folded // 4, folded % 4
        column = jnp.where(row % 2 == 0, column, 3 - column)
        return row * 4 + column + jnp.where(place < 16, 0, 16)
    return place


def ring_place(device, count):
    if count == 8:
        half = device // 2
        return jnp.where(device % 2 == 0, half, 7 - half)
    if count == 32:
        within = device % 16
        row, column = within // 4, within % 4
        column = jnp.where(row % 2 == 0, column, 3 - column)
        folded = row * 4 + column
        return jnp.where(device < 16, folded, 31 - folded)
    return device


def ring_list(count):
    if count == 8:
        return [0, 2, 4, 6, 7, 5, 3, 1]
    if count == 32:
        snake = []
        for row in range(4):
            line = [row * 4 + column for column in range(4)]
            snake += line if row % 2 == 0 else line[::-1]
        return snake + [16 + item for item in reversed(snake)]
    return list(range(count))


def ring_routes(count):
    order = ring_list(count)
    ahead = [(order[i], order[(i + 1) % count]) for i in range(count)]
    return ahead, [(target, source) for source, target in ahead]


def after(value, *earlier):
    return lax.optimization_barrier((value, *earlier))[0]


def tie(values, earlier):
    present = [item for item in values if item is not None]
    if not earlier or not present:
        return values
    tied = list(lax.optimization_barrier((*present, *earlier))[: len(present)])
    return [None if item is None else tied.pop(0) for item in values]


class RingGather:
    def __init__(self, chunk, whole, forward_steps):
        self.count = lax.axis_size("dp")
        self.ahead, self.behind = ring_routes(self.count)
        self.place = ring_place(lax.axis_index("dp"), self.count)
        self.depth = chunk.shape[0]
        self.limits = (forward_steps, self.count - 1 - forward_steps)
        self.steps = max(self.limits)
        self.step = 0
        self.front = self.back = chunk
        self.whole = lax.dynamic_update_slice(
            whole, chunk, (lax.axis_index("dp") * self.depth, 0)
        )

    def put(self, block, distance):
        owner = ring_device((self.place + self.count + distance) % self.count, self.count)
        self.whole = lax.dynamic_update_slice(self.whole, block, (owner * self.depth, 0))

    def advance(self, *earlier):
        self.step += 1
        front = self.front if self.step <= self.limits[0] else None
        back = self.back if self.step <= self.limits[1] else None
        front, back = tie([front, back], earlier)
        if front is not None:
            self.front = lax.ppermute(front, "dp", self.ahead)
            self.put(self.front, -self.step)
        if back is not None:
            self.back = lax.ppermute(back, "dp", self.behind)
            self.put(self.back, self.step)
        return [item for item in (front, back) if item is not None]

    def result(self):
        while self.step < self.steps:
            self.advance()
        return self.whole


class RingScatter:
    def __init__(self, terms, forward_steps):
        self.terms = terms
        self.count = lax.axis_size("dp")
        self.place = ring_place(lax.axis_index("dp"), self.count)
        self.depth = terms.shape[0] // self.count
        self.ahead, self.behind = ring_routes(self.count)
        self.forward_steps = forward_steps
        self.backward_steps = self.count - 1 - forward_steps
        self.steps = max(self.forward_steps, self.backward_steps)
        self.step = 0
        self.front = self.back = None

    def term(self, distance):
        owner = ring_device((self.place + self.count + distance) % self.count, self.count)
        width = self.terms.shape[1]
        return lax.dynamic_slice(self.terms, (owner * self.depth, 0), (self.depth, width))

    def advance(self, *earlier):
        marks = []
        front, back = tie([self.front, self.back], earlier)
        if self.step < self.forward_steps:
            own = self.term(self.forward_steps - self.step)
            if front is not None:
                own = (own.astype(F32) + front.astype(F32)).astype(BF)
            marks.append(own)
            front = lax.ppermute(own, "dp", self.ahead)
        if self.step < self.backward_steps:
            own = self.term(self.step - self.backward_steps)
            if back is not None:
                own = (own.astype(F32) + back.astype(F32)).astype(BF)
            marks.append(own)
            back = lax.ppermute(own, "dp", self.behind)
        self.front, self.back = front, back
        self.step += 1
        return marks

    def result(self):
        while self.step < self.steps:
            self.advance()
        return self.term(0).astype(F32) + self.front.astype(F32) + self.back.astype(F32)


def swap(block, axis):
    return lax.ppermute(block, axis, [(0, 1), (1, 0)])


def dot(left, right):
    return jnp.dot(left, right, preferred_element_type=F32)


def dot_last(left, right):
    return lax.dot_general(left, right, (((1,), (1,)), ((), ())), preferred_element_type=F32)


def dot_first(left, right):
    return lax.dot_general(left, right, (((0,), (0,)), ((), ())), preferred_element_type=F32)


def softmax_rows(queries, keys, bias):
    scores = dot_last(queries, keys) * (1.0 / math.sqrt(HEAD)) + bias
    peak = jnp.max(scores, axis=-1, keepdims=True)
    expons = jnp.exp(scores - peak)
    return expons / jnp.sum(expons, axis=-1, keepdims=True)


def head_parts(packed, index):
    base = index * 3 * HEAD
    return tuple(packed[:, base + j * HEAD : base + (j + 1) * HEAD] for j in range(3))


def turn(values, cosine, upper, lower):
    width = values.shape[1]
    return (
        values * cosine
        + pltpu.roll(values, width - ROT // 2, 1) * upper
        + pltpu.roll(values, ROT // 2, 1) * lower
    )


def pack_kernel(pipe_ref, *refs):
    sources, (kept_ref, sent_ref) = refs[:6], refs[6:8]
    held, marks = refs[10:16], refs[16]
    copies = [
        pltpu.make_async_copy(source, target, marks.at[i])
        for i, (source, target) in enumerate(zip(sources, held))
    ]
    for copy in copies:
        copy.start()
    for copy in copies:
        copy.wait()
    qkv_ref, out_ref, fc_ref, proj_ref = held[:4]
    depth = qkv_ref.shape[0]
    rows = [held[4][...]]
    long_bias = held[5][...]
    qkv_width, out_width = qkv_ref.shape[1] // 2, out_ref.shape[1] // 2
    hidden = fc_ref.shape[1] // 2
    start = qkv_width + out_width
    qkv_bias, fc_bias = long_bias[:, : 2 * qkv_width], long_bias[:, 2 * qkv_width :]

    def fill(target, index):
        target[:, :start] = jnp.concatenate(
            [
                qkv_ref[:, index * qkv_width : (index + 1) * qkv_width],
                out_ref[:, index * out_width : (index + 1) * out_width],
            ],
            axis=1,
        )
        target[:, start : start + hidden] = fc_ref[:, index * hidden : (index + 1) * hidden]
        target[:, start + hidden : start + 2 * hidden] = proj_ref[
            :, index * hidden : (index + 1) * hidden
        ]
        bias = jnp.concatenate(
            [
                qkv_bias[:, index * qkv_width : (index + 1) * qkv_width],
                fc_bias[:, index * hidden : (index + 1) * hidden],
            ],
            axis=1,
        )
        pieces = bias.shape[1] // depth
        small = rows + [bias[:, i * depth : (i + 1) * depth] for i in range(pieces)]
        small.append(jnp.zeros((SMALL - 8 - pieces, depth), F32))
        small = jnp.transpose(jnp.concatenate(small, axis=0))
        target[:, start + 2 * hidden :] = small.astype(BF)

    @pl.when(pipe_ref[0] == 0)
    def _():
        fill(kept_ref, 0)
        fill(sent_ref, 1)

    @pl.when(pipe_ref[0] != 0)
    def _():
        fill(kept_ref, 1)
        fill(sent_ref, 0)


def forward_kernel(
    heads,
    depth,
    own_ref,
    far_ref,
    weight_ref,
    cos_ref,
    upper_ref,
    lower_ref,
    bias_ref,
    mine_ref,
    other_ref,
    low_ref,
    high_ref,
    vector_ref,
):
    rows, model = own_ref.shape
    qkv_width = heads * 3 * HEAD
    start = heads * 4 * HEAD
    wide = cos_ref.shape[1]
    hidden = high_ref.shape[1] - model - 128
    pieces = (qkv_width + hidden) // depth
    small = jnp.transpose(weight_ref[:, start + 2 * hidden :].astype(F32))
    vectors = small[:8]
    vector_ref[...] = vectors
    long_bias = jnp.concatenate([small[8 + i : 9 + i, :depth] for i in range(pieces)], axis=1)
    qkv_bias = jnp.concatenate(
        [long_bias[:, :qkv_width], jnp.zeros((1, wide - qkv_width), F32)], axis=1
    )
    fc_bias = long_bias[:, qkv_width:]
    values = jnp.concatenate([own_ref[...], far_ref[...]], axis=0).astype(F32)
    centred = values - jnp.mean(values, axis=-1, keepdims=True)
    scale = lax.rsqrt(jnp.mean(centred * centred, axis=-1, keepdims=True) + EPSILON)
    xhat = centred * scale
    high_ref[:, :model] = xhat
    high_ref[:, model + hidden :] = jnp.broadcast_to(scale, (2 * rows, 128))
    first = (xhat * vectors[0:1] + vectors[1:2]).astype(BF)
    second = (xhat * vectors[2:3] + vectors[3:4]).astype(BF)
    low_ref[:, :model] = first
    low_ref[:, model : 2 * model] = second
    packed = dot(first, weight_ref[:, :wide]) + qkv_bias
    packed = turn(packed, cos_ref[...], upper_ref[...], lower_ref[...]).astype(BF)
    spot = low_ref.shape[1] - wide
    low_ref[:, spot:] = packed
    bias = bias_ref[...]
    mixed = []
    for index in range(heads):
        queries, keys, held = head_parts(packed, index)
        weights = softmax_rows(queries, keys, bias).astype(BF)
        mixed.append(dot(weights, held))
    mixed = jnp.concatenate(mixed, axis=1).astype(BF)
    tail = spot - 2 * model - hidden - mixed.shape[1]
    low_ref[:, 2 * model + hidden : spot] = (
        jnp.concatenate([mixed, jnp.zeros((2 * rows, tail), BF)], axis=1) if tail else mixed
    )
    pre = dot(second, weight_ref[:, start : start + hidden]) + fc_bias
    high_ref[:, model : model + hidden] = pre
    act = (pre * (0.5 + 0.5 * lax.erf(pre * math.sqrt(0.5)))).astype(BF)
    low_ref[:, 2 * model : 2 * model + hidden] = act
    total = dot_last(act, weight_ref[:, start + hidden : start + 2 * hidden])
    total = total + dot_last(mixed, weight_ref[:, qkv_width:start])
    mine_ref[...] = total[:rows]
    other_ref[...] = total[rows:]


def backward_kernel(
    heads,
    own_ref,
    far_ref,
    weight_ref,
    cos_ref,
    upper_ref,
    lower_ref,
    bias_ref,
    low_ref,
    high_ref,
    vector_ref,
    mine_ref,
    other_ref,
    d_packed_ref,
    d_pre_ref,
    sums_ref,
):
    rows, model = own_ref.shape
    qkv_width = heads * 3 * HEAD
    start = heads * 4 * HEAD
    wide = cos_ref.shape[1]
    hidden = high_ref.shape[1] - model - 128
    grad = jnp.concatenate([own_ref[...], far_ref[...]], axis=0)
    d_act = dot(grad, weight_ref[:, start + hidden : start + 2 * hidden])
    pre = high_ref[:, model : model + hidden]
    slope = 0.5 + 0.5 * lax.erf(pre * math.sqrt(0.5))
    slope = slope + pre * (jnp.exp(pre * pre * -0.5) * (1.0 / math.sqrt(2.0 * math.pi)))
    d_pre = (d_act * slope).astype(BF)
    d_pre_ref[...] = d_pre
    d_second = dot_last(d_pre, weight_ref[:, start : start + hidden])
    d_mixed = dot(grad, weight_ref[:, qkv_width:start]).astype(BF)
    bias = bias_ref[...]
    packed = low_ref[:, low_ref.shape[1] - wide :]
    parts = []
    for index in range(heads):
        queries, keys, held = head_parts(packed, index)
        weights = softmax_rows(queries, keys, bias)
        given = d_mixed[:, index * HEAD : (index + 1) * HEAD]
        d_held = dot_first(weights.astype(BF), given)
        d_weights = dot_last(given, held)
        row_dot = jnp.sum(weights * d_weights, axis=-1, keepdims=True)
        d_scores = (weights * (d_weights - row_dot)).astype(BF)
        parts.append(dot(d_scores, keys) * (1.0 / math.sqrt(HEAD)))
        parts.append(dot_first(d_scores, queries) * (1.0 / math.sqrt(HEAD)))
        parts.append(d_held)
    if wide > qkv_width:
        parts.append(jnp.zeros((2 * rows, wide - qkv_width), F32))
    d_packed = jnp.concatenate(parts, axis=1)
    d_packed = turn(d_packed, cos_ref[...], -upper_ref[...], -lower_ref[...]).astype(BF)
    d_packed_ref[...] = d_packed
    d_first = dot_last(d_packed, weight_ref[:, :wide])
    xhat = high_ref[:, :model]
    inner = d_first * vector_ref[0:1] + d_second * vector_ref[2:3]
    average = jnp.mean(inner, axis=-1, keepdims=True)
    along = jnp.mean(inner * xhat, axis=-1, keepdims=True)
    total = (inner - average - xhat * along) * high_ref[:, model + hidden : model + hidden + 1]
    mine_ref[...] = total[:rows]
    other_ref[...] = total[rows:]

    def add_rows(block):
        return jnp.sum(block, axis=0, keepdims=True)

    width = sums_ref.shape[1]
    packed_sum = add_rows(d_packed.astype(F32))
    if wide < width:
        packed_sum = jnp.concatenate([packed_sum, jnp.zeros((1, width - wide), F32)], axis=1)
    sums_ref[...] = jnp.concatenate(
        [
            add_rows(d_first * xhat),
            add_rows(d_first),
            add_rows(d_second * xhat),
            add_rows(d_second),
            add_rows(grad.astype(F32)) * 0.25,
            add_rows(d_pre.astype(F32)),
            packed_sum,
            jnp.zeros((1, width), F32),
        ],
        axis=0,
    )


def weight_kernel(heads, depth, count, *refs):
    refs = list(refs)
    groups = [refs[i * 9 : (i + 1) * 9] for i in range(count)]
    terms_ref, full_refs = refs[10 * count], refs[9 * count : 10 * count]
    qkv_width = heads * 3 * HEAD
    start = heads * 4 * HEAD
    tile = terms_ref.shape[0]

    def both(index):
        return jnp.concatenate([group[index][...] for group in groups], axis=0)

    def both_grads():
        parts = []
        for group in groups:
            parts += [group[2][...], group[3][...]]
        return jnp.concatenate(parts, axis=0)

    first, second, grad = both(0), both(1), both_grads()
    d_packed, d_pre, mixed, act = both(4), both(5), both(6), both(7)
    hidden = d_pre.shape[1]
    sums = sum(group[8][...] for group in groups[1:]) + groups[0][8][...]
    full = sum(item[...] for item in full_refs[1:]) + full_refs[0][...]
    long_row = jnp.concatenate([full[6:7, :qkv_width], full[5:6, :hidden]], axis=1)
    pieces = long_row.shape[1] // depth
    stacked = jnp.concatenate(
        [long_row[:, i * depth : (i + 1) * depth] for i in range(pieces)], axis=0
    )
    stacked = jnp.concatenate([stacked] * (tile // depth), axis=1)
    rest = SMALL - 8 - pieces
    small = jnp.concatenate([sums, stacked, jnp.zeros((rest, tile), F32)], axis=0)
    terms_ref[:, :start] = jnp.concatenate(
        [dot_first(first, d_packed)[:, :qkv_width], dot_first(grad, mixed)[:, : heads * HEAD]], axis=1
    ).astype(BF)
    terms_ref[:, start : start + hidden] = dot_first(second, d_pre).astype(BF)
    terms_ref[:, start + hidden : start + 2 * hidden] = dot_first(grad, act).astype(BF)
    terms_ref[:, start + 2 * hidden :] = jnp.transpose(small).astype(BF)


def unpack_kernel(
    pipe_ref,
    own_ref,
    came_ref,
    own_small_ref,
    came_small_ref,
    qkv_ref,
    qkv_bias_ref,
    out_ref,
    fc_ref,
    fc_bias_ref,
    proj_ref,
    *vector_refs,
):
    depth = qkv_ref.shape[0]
    qkv_width, out_width = qkv_ref.shape[1] // 2, out_ref.shape[1] // 2
    hidden = fc_ref.shape[1] // 2
    start = qkv_width + out_width
    pieces = (qkv_width + hidden) // depth
    smalls = [jnp.transpose(ref[...]) for ref in (own_small_ref, came_small_ref)]
    vectors = smalls[0][:8] + smalls[1][:8]
    for index, ref in enumerate(vector_refs):
        ref[...] = vectors[index : index + 1]
    longs = [
        jnp.concatenate([small[8 + i : 9 + i] for i in range(pieces)], axis=1) for small in smalls
    ]

    def fill(lower, upper, low_bias, high_bias):
        for index, (block, bias) in enumerate(((lower, low_bias), (upper, high_bias))):
            columns = slice(index * qkv_width, (index + 1) * qkv_width)
            qkv_ref[:, columns] = block[:, :qkv_width].astype(F32)
            qkv_bias_ref[:, columns] = bias[:, :qkv_width]
            lines = slice(index * out_width, (index + 1) * out_width)
            out_ref[:, lines] = block[:, qkv_width:start].astype(F32)
            units = slice(index * hidden, (index + 1) * hidden)
            fc_ref[:, units] = block[:, start : start + hidden].astype(F32)
            fc_bias_ref[:, units] = bias[:, qkv_width:]
            proj_ref[:, units] = block[:, start + hidden : start + 2 * hidden].astype(F32)

    @pl.when(pipe_ref[0] == 0)
    def _():
        fill(own_ref, came_ref, longs[0], longs[1])

    @pl.when(pipe_ref[0] != 0)
    def _():
        fill(came_ref, own_ref, longs[1], longs[0])


def cost(flops, moved):
    return pl.CostEstimate(flops=int(flops), bytes_accessed=int(moved), transcendentals=0)


def mixed_width(heads):
    return heads * HEAD + -(heads * HEAD) % 128


def in_vmem():
    return pl.BlockSpec(memory_space=pltpu.VMEM)


def pack_call(pipe, arrays, count):
    qkv, out, fc = arrays[:3]
    width = (qkv.shape[1] + out.shape[1]) // 2 + fc.shape[1] + SMALL
    packet = jax.ShapeDtypeStruct((qkv.shape[0], width), BF)
    whole = jax.ShapeDtypeStruct((count * qkv.shape[0], width), BF)
    return pl.pallas_call(
        pack_kernel,
        out_shape=(packet, packet, whole, whole),
        out_specs=(in_vmem(),) * 4,
        in_specs=[pl.BlockSpec(memory_space=pltpu.SMEM)]
        + [pl.BlockSpec(memory_space=pl.ANY)] * len(arrays),
        scratch_shapes=[pltpu.VMEM(item.shape, item.dtype) for item in arrays]
        + [pltpu.SemaphoreType.DMA((len(arrays),))],
        compiler_params=pltpu.CompilerParams(vmem_limit_bytes=VMEM_LIMIT),
        cost_estimate=cost(0, 4e6),
        name="pack",
    )(pipe, *arrays)


def unpack_call(pipe, own, came, own_small, came_small, widths):
    depth = own.shape[0]
    qkv_width, out_width, hidden = widths
    shapes = (
        (depth, 2 * qkv_width),
        (1, 2 * qkv_width),
        (depth, 2 * out_width),
        (depth, 2 * hidden),
        (1, 2 * hidden),
        (depth, 2 * hidden),
    ) + ((1, depth),) * 5
    return pl.pallas_call(
        unpack_kernel,
        out_shape=tuple(jax.ShapeDtypeStruct(shape, F32) for shape in shapes),
        in_specs=[pl.BlockSpec(memory_space=pltpu.SMEM)] + [in_vmem()] * 4,
        compiler_params=pltpu.CompilerParams(vmem_limit_bytes=VMEM_LIMIT),
        cost_estimate=cost(0, 6e6),
        name="unpack",
    )(pipe, own, came, own_small, came_small)


def forward_call(own, far, weight, layout, heads, hidden, depth):
    rows, model = own.shape
    full = 2 * rows
    wide = layout[0].shape[1]

    def shape(height, width, kind):
        return jax.ShapeDtypeStruct((height, width), kind)

    outs = (
        shape(rows, model, F32),
        shape(rows, model, F32),
        shape(full, 2 * model + hidden + mixed_width(heads) + wide, BF),
        shape(full, model + hidden + 128, F32),
        shape(8, model, F32),
    )
    return pl.pallas_call(
        functools.partial(forward_kernel, heads, depth),
        out_shape=outs,
        compiler_params=pltpu.CompilerParams(vmem_limit_bytes=VMEM_LIMIT),
        cost_estimate=cost(4e9, 8e6),
        name="forward",
    )(own, far, weight, *layout)


def backward_call(own, far, weight, layout, kept, heads):
    rows, model = own.shape
    full = 2 * rows
    wide = layout[0].shape[1]
    low, high, vectors = kept
    hidden = high.shape[1] - model - 128
    outs = (
        jax.ShapeDtypeStruct((rows, model), F32),
        jax.ShapeDtypeStruct((rows, model), F32),
        jax.ShapeDtypeStruct((full, wide), BF),
        jax.ShapeDtypeStruct((full, hidden), BF),
        jax.ShapeDtypeStruct((8, model), F32),
    )
    return pl.pallas_call(
        functools.partial(backward_kernel, heads),
        out_shape=outs,
        compiler_params=pltpu.CompilerParams(vmem_limit_bytes=VMEM_LIMIT),
        cost_estimate=cost(5e9, 10e6),
        name="backward",
    )(own, far, weight, *layout, low, high, vectors)


def weight_call(grads, kept, backs, heads, depth):
    model = grads[0][0].shape[1]
    hidden = kept[0][1].shape[1] - model - 128
    tile = model // 2
    mixed = mixed_width(heads)
    width = heads * 4 * HEAD + 2 * hidden + SMALL
    operands, specs = [], []

    def tiled(array, first=0):
        operands.append(array)
        specs.append(pl.BlockSpec((array.shape[0], tile), lambda i: (0, first + i)))

    def part(array, start, width):
        operands.append(array)
        specs.append(pl.BlockSpec((array.shape[0], width), lambda i: (0, start // width)))

    def whole(array):
        operands.append(array)
        specs.append(pl.BlockSpec(array.shape, lambda i: (0, 0)))

    for (own, far), keep, back in zip(grads, kept, backs):
        tiled(keep[0])
        tiled(keep[0], 2)
        tiled(own)
        tiled(far)
        whole(back[2])
        whole(back[3])
        part(keep[0], 2 * model + hidden, mixed)
        part(keep[0], 2 * model, hidden)
        tiled(back[4])
    for back in backs:
        whole(back[4])
    return pl.pallas_call(
        functools.partial(weight_kernel, heads, depth, len(grads)),
        grid=(2,),
        in_specs=specs,
        out_specs=pl.BlockSpec((tile, width), lambda i: (i, 0)),
        out_shape=jax.ShapeDtypeStruct((model, width), BF),
        compiler_params=pltpu.CompilerParams(vmem_limit_bytes=VMEM_LIMIT),
        cost_estimate=cost(8e9, 10e6),
        name="weights",
    )(*operands)


def layout_of(lengths, rows, first_row, heads):
    full = 2 * rows
    ends = jnp.cumsum(lengths)
    places = (jnp.arange(full, dtype=jnp.int32) + first_row) % full
    segment = jnp.sum((places[:, None] >= ends[None, :]).astype(jnp.int32), axis=1)
    picked = segment[:, None] == jnp.arange(lengths.shape[0], dtype=jnp.int32)[None, :]
    position = places - jnp.sum(jnp.where(picked, (ends - lengths)[None, :], 0), axis=1)
    allowed = (segment[:, None] == segment[None, :]) & (places[:, None] >= places[None, :])
    bias = jnp.where(allowed, 0.0, NEG_BIG).astype(F32)
    half = ROT // 2
    inverse = jnp.exp(jnp.arange(half, dtype=F32) * (-2.0 * math.log(10000.0) / ROT))
    angles = position.astype(F32)[:, None] * inverse
    cosine, sine = jnp.cos(angles), jnp.sin(angles)
    plain = jnp.ones((full, HEAD - ROT), F32)
    empty = jnp.zeros((full, HEAD - ROT), F32)
    none = jnp.zeros((full, half), F32)
    cos_head = jnp.concatenate([cosine, cosine, plain], axis=1)
    upper_head = jnp.concatenate([-sine, none, empty], axis=1)
    lower_head = jnp.concatenate([none, sine, empty], axis=1)

    def spread(head, fill):
        rest = jnp.full((full, HEAD), fill, F32)
        table = jnp.concatenate([head, head, rest] * heads, axis=1)
        pad = -table.shape[1] % 128
        return jnp.concatenate([table, jnp.full((full, pad), fill, F32)], axis=1) if pad else table

    return spread(cos_head, 1.0), spread(upper_head, 0.0), spread(lower_head, 0.0), bias


def local(
    inputs,
    lengths,
    ln1_gain,
    ln1_shift,
    ln2_gain,
    ln2_shift,
    qkv_weight,
    qkv_bias,
    out_weight,
    fc_weight,
    fc_bias,
    proj_weight,
    branch_bias,
    cotangent,
):
    micro, rows, model = inputs.shape
    count = lax.axis_size("dp")
    pipe = lax.axis_index("pipe")
    core = lax.axis_index("tensor")
    leading = pipe == 0
    depth = qkv_weight.shape[1]
    qkv_width = qkv_weight.shape[2] // 2
    out_width = out_weight.shape[1] // 2
    hidden = fc_weight.shape[2] // 2
    heads = out_width // HEAD
    ahead_steps = count // 2

    pipe_word = pipe.astype(jnp.int32).reshape(1)
    vectors = jnp.concatenate([ln1_gain, ln1_shift, ln2_gain, ln2_shift, branch_bias], axis=0)
    vectors = jnp.pad(vectors.astype(F32), ((0, 3), (0, 0)))
    kept_part, sent_part, first_whole, second_whole = pack_call(
        pipe_word,
        (
            qkv_weight[0],
            jnp.transpose(out_weight[0]),
            fc_weight[0],
            jnp.transpose(proj_weight[0]),
            vectors,
            jnp.concatenate([qkv_bias, fc_bias], axis=1).astype(F32),
        ),
        count,
    )
    came_part = swap(sent_part, "pipe")
    chunk = jnp.where(leading, kept_part, came_part)
    gather = RingGather(chunk, first_whole, ahead_steps)
    later = RingGather(
        jnp.where(leading, came_part, kept_part), second_whole, count - 1 - ahead_steps
    )
    gather.advance()
    order = later.advance()
    while gather.step < gather.steps or later.step < later.steps:
        if gather.step < gather.steps:
            order = gather.advance(*order)
        if later.step < later.steps:
            order = later.advance(*order)
    weights = [gather.result(), later.result()]

    lengths = after(lengths, chunk)
    inputs, cotangent = after(inputs, sent_part), after(cotangent, chunk)
    layouts = [layout_of(lengths[m, 0], rows, core * rows, heads) for m in range(micro)]

    def complete(half, base):
        came = swap(half, "pipe")
        return (base + (half.astype(F32) + came.astype(F32))).astype(BF)

    def half_sum(mine, other):
        return (mine + swap(other, "tensor")).astype(BF)

    current = [(inputs[m], swap(inputs[m], "tensor")) for m in range(micro)]
    cotangents = [(cotangent[m], swap(cotangent[m], "tensor")) for m in range(micro)]
    stored, outputs = [], []
    for section in range(2):
        kept_rows, results = [], []
        for m in range(micro):
            own, far = current[m]
            found = forward_call(own, far, weights[section], layouts[m], heads, hidden, depth)
            kept_rows.append(found[2:])
            half = half_sum(found[0], found[1])
            base = own.astype(F32) + found[-1][4:5]
            results.append(complete(half, base))
        if section == 0:
            current = [(item, swap(item, "tensor")) for item in results]
        stored.append(kept_rows)
        outputs.append(results)

    back_outputs = [None, None]
    backs, results, halves = [], [], []
    for m in range(micro):
        own, far = cotangents[m]
        found = backward_call(own, far, weights[1], layouts[m], stored[1][m], heads)
        backs.append(found)
        halves.append(half_sum(found[0], found[1]))
        results.append(complete(halves[m], own.astype(F32)))
    back_outputs[1] = results
    grads = [(item, swap(item, "tensor")) for item in results]
    backs[-1] = (*backs[-1][:4], after(backs[-1][4], halves[-1]))
    scatter = RingScatter(weight_call(cotangents, stored[1], backs, heads, depth), ahead_steps)
    scatter.advance()
    backs, results, marks = [], [], ()
    for m in range(micro):
        own, far = grads[m]
        if marks:
            own = after(own, marks[-1])
        found = backward_call(own, far, weights[0], layouts[m], stored[0][m], heads)
        backs.append(found)
        results.append(complete(half_sum(found[0], found[1]), own.astype(F32)))
        if m + 1 < micro:
            marks = scatter.advance(found[4])
    back_outputs[0] = results
    backs[-1] = (*backs[-1][:4], after(backs[-1][4], *marks[:TIES]))
    terms = weight_call(grads, stored[0], backs, heads, depth)
    last = RingScatter(terms, count - 1 - ahead_steps)
    order = last.advance()
    while scatter.step < scatter.steps or last.step < last.steps:
        if scatter.step < scatter.steps:
            order = scatter.advance(*order[:TIES])
        if last.step < last.steps:
            order = last.advance(*order[:TIES])
    reduced = [last.result(), scatter.result()]

    activations = jnp.where(leading, jnp.stack(outputs[0]), jnp.stack(outputs[1]))[None]
    input_grads = jnp.where(leading, jnp.stack(back_outputs[0]), jnp.stack(back_outputs[1]))[None]

    start = qkv_width + out_width
    own_part = jnp.where(leading, reduced[0], reduced[1])
    given_part = jnp.where(leading, reduced[1], reduced[0])
    came_part = swap(given_part[:, : start + 2 * hidden].astype(BF), "pipe")
    smalls = jnp.concatenate(
        [own_part[:, start + 2 * hidden :], given_part[:, start + 2 * hidden :]], axis=0
    )
    lane = lax.broadcasted_iota(jnp.int32, smalls.shape, 1)
    smalls = jnp.where(lane < 8, smalls + swap(smalls, "tensor"), smalls)
    came_small = swap(smalls[depth:], "pipe")
    grads_out = unpack_call(
        pipe_word, own_part, came_part, smalls[:depth], came_small, (qkv_width, out_width, hidden)
    )
    qkv_grad, qkv_bias_grad, out_grad, fc_grad, fc_bias_grad, proj_grad = grads_out[:6]
    vector_grads = grads_out[6:]
    return (
        activations,
        input_grads,
        vector_grads[0],
        vector_grads[1],
        vector_grads[2],
        vector_grads[3],
        qkv_grad[None],
        qkv_bias_grad,
        jnp.transpose(out_grad)[None],
        fc_grad[None],
        fc_bias_grad,
        jnp.transpose(proj_grad)[None],
        vector_grads[4],
    )


def solution(mesh):
    rows = P(None, ("dp", "tensor"), None)
    vector = P("pipe", "dp")
    bias = P("pipe", "tensor")
    wide = P("pipe", "dp", "tensor")
    tall = P("pipe", "tensor", "dp")
    result = P("pipe", None, ("dp", "tensor"), None)
    return jax.shard_map(
        local,
        mesh=mesh,
        in_specs=(
            rows,
            P(None, "dp", None),
            vector,
            vector,
            vector,
            vector,
            wide,
            bias,
            tall,
            wide,
            bias,
            tall,
            vector,
            rows,
        ),
        out_specs=(
            result,
            result,
            vector,
            vector,
            vector,
            vector,
            wide,
            bias,
            tall,
            wide,
            bias,
            tall,
            vector,
        ),
        check_vma=False,
    )
```

```python
import functools
import math

import jax
import jax.numpy as jnp
from jax import lax
from jax.experimental import pallas as pl
from jax.experimental.pallas import tpu as pltpu
from jax.sharding import PartitionSpec as P

HEAD = 64
ROT = 16
EPSILON = 1e-05
NEG_BIG = -1e30
VMEM_LIMIT = 16 * 1024 * 1024
BF = jnp.bfloat16
F32 = jnp.float32
SMALL = 128
TIES = 2


def ring_device(place, count):
    if count == 8:
        return jnp.where(place < 4, 2 * place, 15 - 2 * place)
    if count == 32:
        folded = jnp.where(place < 16, place, 31 - place)
        row, column = folded // 4, folded % 4
        column = jnp.where(row % 2 == 0, column, 3 - column)
        return row * 4 + column + jnp.where(place < 16, 0, 16)
    return place


def ring_place(device, count):
    if count == 8:
        half = device // 2
        return jnp.where(device % 2 == 0, half, 7 - half)
    if count == 32:
        within = device % 16
        row, column = within // 4, within % 4
        column = jnp.where(row % 2 == 0, column, 3 - column)
        folded = row * 4 + column
        return jnp.where(device < 16, folded, 31 - folded)
    return device


def ring_list(count):
    if count == 8:
        return [0, 2, 4, 6, 7, 5, 3, 1]
    if count == 32:
        snake = []
        for row in range(4):
            line = [row * 4 + column for column in range(4)]
            snake += line if row % 2 == 0 else line[::-1]
        return snake + [16 + item for item in reversed(snake)]
    return list(range(count))


def ring_routes(count):
    order = ring_list(count)
    ahead = [(order[i], order[(i + 1) % count]) for i in range(count)]
    return ahead, [(target, source) for source, target in ahead]


def after(value, *earlier):
    return lax.optimization_barrier((value, *earlier))[0]


def tie(values, earlier):
    present = [item for item in values if item is not None]
    if not earlier or not present:
        return values
    tied = list(lax.optimization_barrier((*present, *earlier))[: len(present)])
    return [None if item is None else tied.pop(0) for item in values]


def blank_kernel(like_ref, whole_ref):
    whole_ref[:16, :] = jnp.zeros((16, whole_ref.shape[1]), whole_ref.dtype)


def blank_call(like, count):
    return pl.pallas_call(
        blank_kernel,
        out_shape=jax.ShapeDtypeStruct((count * like.shape[0], like.shape[1]), like.dtype),
        compiler_params=pltpu.CompilerParams(vmem_limit_bytes=VMEM_LIMIT),
        cost_estimate=cost(0, 1e5),
        name="blank",
    )(like)


class RingGather:
    def __init__(self, chunk, whole, forward_steps):
        self.count = lax.axis_size("dp")
        self.ahead, self.behind = ring_routes(self.count)
        self.place = ring_place(lax.axis_index("dp"), self.count)
        self.depth = chunk.shape[0]
        self.limits = (forward_steps, self.count - 1 - forward_steps)
        self.steps = max(self.limits)
        self.step = 0
        self.front = self.back = chunk
        self.whole = lax.dynamic_update_slice(
            whole, chunk, (lax.axis_index("dp") * self.depth, 0)
        )

    def put(self, block, distance):
        owner = ring_device((self.place + self.count + distance) % self.count, self.count)
        self.whole = lax.dynamic_update_slice(self.whole, block, (owner * self.depth, 0))

    def advance(self, *earlier):
        self.step += 1
        front = self.front if self.step <= self.limits[0] else None
        back = self.back if self.step <= self.limits[1] else None
        front, back = tie([front, back], earlier)
        if front is not None:
            self.front = lax.ppermute(front, "dp", self.ahead)
            self.put(self.front, -self.step)
        if back is not None:
            self.back = lax.ppermute(back, "dp", self.behind)
            self.put(self.back, self.step)
        return [item for item in (front, back) if item is not None]

    def result(self):
        while self.step < self.steps:
            self.advance()
        return self.whole


class RingScatter:
    def __init__(self, terms, forward_steps):
        self.terms = terms
        self.count = lax.axis_size("dp")
        self.place = ring_place(lax.axis_index("dp"), self.count)
        self.depth = terms.shape[0] // self.count
        self.ahead, self.behind = ring_routes(self.count)
        self.forward_steps = forward_steps
        self.backward_steps = self.count - 1 - forward_steps
        self.steps = max(self.forward_steps, self.backward_steps)
        self.step = 0
        self.front = self.back = None

    def term(self, distance):
        owner = ring_device((self.place + self.count + distance) % self.count, self.count)
        width = self.terms.shape[1]
        return lax.dynamic_slice(self.terms, (owner * self.depth, 0), (self.depth, width))

    def advance(self, *earlier):
        marks = []
        front, back = tie([self.front, self.back], earlier)
        if self.step < self.forward_steps:
            own = self.term(self.forward_steps - self.step)
            if front is not None:
                own = (own.astype(F32) + front.astype(F32)).astype(BF)
            marks.append(own)
            front = lax.ppermute(own, "dp", self.ahead)
        if self.step < self.backward_steps:
            own = self.term(self.step - self.backward_steps)
            if back is not None:
                own = (own.astype(F32) + back.astype(F32)).astype(BF)
            marks.append(own)
            back = lax.ppermute(own, "dp", self.behind)
        self.front, self.back = front, back
        self.step += 1
        return marks

    def result(self):
        while self.step < self.steps:
            self.advance()
        return self.term(0).astype(F32) + self.front.astype(F32) + self.back.astype(F32)


def swap(block, axis):
    return lax.ppermute(block, axis, [(0, 1), (1, 0)])


def dot(left, right):
    return jnp.dot(left, right, preferred_element_type=F32)


def dot_last(left, right):
    return lax.dot_general(left, right, (((1,), (1,)), ((), ())), preferred_element_type=F32)


def dot_first(left, right):
    return lax.dot_general(left, right, (((0,), (0,)), ((), ())), preferred_element_type=F32)


def softmax_rows(queries, keys, bias):
    scores = dot_last(queries, keys) * (1.0 / math.sqrt(HEAD)) + bias
    peak = jnp.max(scores, axis=-1, keepdims=True)
    expons = jnp.exp(scores - peak)
    return expons / jnp.sum(expons, axis=-1, keepdims=True)


def head_parts(packed, index):
    base = index * 3 * HEAD
    return tuple(packed[:, base + j * HEAD : base + (j + 1) * HEAD] for j in range(3))


def turn(values, cosine, upper, lower):
    width = values.shape[1]
    return (
        values * cosine
        + pltpu.roll(values, width - ROT // 2, 1) * upper
        + pltpu.roll(values, ROT // 2, 1) * lower
    )


def pack_kernel(pipe_ref, *refs):
    sources, (kept_ref, sent_ref) = refs[:6], refs[6:8]
    held, marks = refs[8:14], refs[14]
    copies = [
        pltpu.make_async_copy(source, target, marks.at[i])
        for i, (source, target) in enumerate(zip(sources, held))
    ]
    for copy in copies:
        copy.start()
    for copy in copies:
        copy.wait()
    qkv_ref, out_ref, fc_ref, proj_ref = held[:4]
    depth = qkv_ref.shape[0]
    rows = [held[4][...]]
    long_bias = held[5][...]
    qkv_width, out_width = qkv_ref.shape[1] // 2, out_ref.shape[1] // 2
    hidden = fc_ref.shape[1] // 2
    start = qkv_width + out_width
    qkv_bias, fc_bias = long_bias[:, : 2 * qkv_width], long_bias[:, 2 * qkv_width :]

    def fill(target, index):
        target[:, :start] = jnp.concatenate(
            [
                qkv_ref[:, index * qkv_width : (index + 1) * qkv_width],
                out_ref[:, index * out_width : (index + 1) * out_width],
            ],
            axis=1,
        )
        target[:, start : start + hidden] = fc_ref[:, index * hidden : (index + 1) * hidden]
        target[:, start + hidden : start + 2 * hidden] = proj_ref[
            :, index * hidden : (index + 1) * hidden
        ]
        bias = jnp.concatenate(
            [
                qkv_bias[:, index * qkv_width : (index + 1) * qkv_width],
                fc_bias[:, index * hidden : (index + 1) * hidden],
            ],
            axis=1,
        )
        pieces = bias.shape[1] // depth
        small = rows + [bias[:, i * depth : (i + 1) * depth] for i in range(pieces)]
        small.append(jnp.zeros((SMALL - 8 - pieces, depth), F32))
        small = jnp.transpose(jnp.concatenate(small, axis=0))
        target[:, start + 2 * hidden :] = small.astype(BF)

    @pl.when(pipe_ref[0] == 0)
    def _():
        fill(kept_ref, 0)
        fill(sent_ref, 1)

    @pl.when(pipe_ref[0] != 0)
    def _():
        fill(kept_ref, 1)
        fill(sent_ref, 0)


def forward_kernel(
    heads,
    depth,
    own_ref,
    far_ref,
    weight_ref,
    cos_ref,
    upper_ref,
    lower_ref,
    bias_ref,
    mine_ref,
    other_ref,
    low_ref,
    high_ref,
    vector_ref,
):
    rows, model = own_ref.shape
    qkv_width = heads * 3 * HEAD
    start = heads * 4 * HEAD
    wide = cos_ref.shape[1]
    hidden = high_ref.shape[1] - model - 128
    pieces = (qkv_width + hidden) // depth
    small = jnp.transpose(weight_ref[:, start + 2 * hidden :].astype(F32))
    vectors = small[:8]
    vector_ref[...] = vectors
    long_bias = jnp.concatenate([small[8 + i : 9 + i, :depth] for i in range(pieces)], axis=1)
    qkv_bias = jnp.concatenate(
        [long_bias[:, :qkv_width], jnp.zeros((1, wide - qkv_width), F32)], axis=1
    )
    fc_bias = long_bias[:, qkv_width:]
    values = jnp.concatenate([own_ref[...], far_ref[...]], axis=0).astype(F32)
    centred = values - jnp.mean(values, axis=-1, keepdims=True)
    scale = lax.rsqrt(jnp.mean(centred * centred, axis=-1, keepdims=True) + EPSILON)
    xhat = centred * scale
    high_ref[:, :model] = xhat
    high_ref[:, model + hidden :] = jnp.broadcast_to(scale, (2 * rows, 128))
    first = (xhat * vectors[0:1] + vectors[1:2]).astype(BF)
    second = (xhat * vectors[2:3] + vectors[3:4]).astype(BF)
    low_ref[:, :model] = first
    low_ref[:, model : 2 * model] = second
    packed = dot(first, weight_ref[:, :wide]) + qkv_bias
    packed = turn(packed, cos_ref[...], upper_ref[...], lower_ref[...]).astype(BF)
    spot = low_ref.shape[1] - wide
    low_ref[:, spot:] = packed
    bias = bias_ref[...]
    mixed = []
    for index in range(heads):
        queries, keys, held = head_parts(packed, index)
        weights = softmax_rows(queries, keys, bias).astype(BF)
        mixed.append(dot(weights, held))
    mixed = jnp.concatenate(mixed, axis=1).astype(BF)
    tail = spot - 2 * model - hidden - mixed.shape[1]
    low_ref[:, 2 * model + hidden : spot] = (
        jnp.concatenate([mixed, jnp.zeros((2 * rows, tail), BF)], axis=1) if tail else mixed
    )
    pre = dot(second, weight_ref[:, start : start + hidden]) + fc_bias
    high_ref[:, model : model + hidden] = pre
    act = (pre * (0.5 + 0.5 * lax.erf(pre * math.sqrt(0.5)))).astype(BF)
    low_ref[:, 2 * model : 2 * model + hidden] = act
    total = dot_last(act, weight_ref[:, start + hidden : start + 2 * hidden])
    total = total + dot_last(mixed, weight_ref[:, qkv_width:start])
    mine_ref[...] = total[:rows]
    other_ref[...] = total[rows:]


def backward_kernel(
    heads,
    own_ref,
    far_ref,
    weight_ref,
    cos_ref,
    upper_ref,
    lower_ref,
    bias_ref,
    low_ref,
    high_ref,
    vector_ref,
    mine_ref,
    other_ref,
    d_packed_ref,
    d_pre_ref,
    sums_ref,
):
    rows, model = own_ref.shape
    qkv_width = heads * 3 * HEAD
    start = heads * 4 * HEAD
    wide = cos_ref.shape[1]
    hidden = high_ref.shape[1] - model - 128
    grad = jnp.concatenate([own_ref[...], far_ref[...]], axis=0)
    d_act = dot(grad, weight_ref[:, start + hidden : start + 2 * hidden])
    pre = high_ref[:, model : model + hidden]
    slope = 0.5 + 0.5 * lax.erf(pre * math.sqrt(0.5))
    slope = slope + pre * (jnp.exp(pre * pre * -0.5) * (1.0 / math.sqrt(2.0 * math.pi)))
    d_pre = (d_act * slope).astype(BF)
    d_pre_ref[...] = d_pre
    d_second = dot_last(d_pre, weight_ref[:, start : start + hidden])
    d_mixed = dot(grad, weight_ref[:, qkv_width:start]).astype(BF)
    bias = bias_ref[...]
    packed = low_ref[:, low_ref.shape[1] - wide :]
    parts = []
    for index in range(heads):
        queries, keys, held = head_parts(packed, index)
        weights = softmax_rows(queries, keys, bias)
        given = d_mixed[:, index * HEAD : (index + 1) * HEAD]
        d_held = dot_first(weights.astype(BF), given)
        d_weights = dot_last(given, held)
        row_dot = jnp.sum(weights * d_weights, axis=-1, keepdims=True)
        d_scores = (weights * (d_weights - row_dot)).astype(BF)
        parts.append(dot(d_scores, keys) * (1.0 / math.sqrt(HEAD)))
        parts.append(dot_first(d_scores, queries) * (1.0 / math.sqrt(HEAD)))
        parts.append(d_held)
    if wide > qkv_width:
        parts.append(jnp.zeros((2 * rows, wide - qkv_width), F32))
    d_packed = jnp.concatenate(parts, axis=1)
    d_packed = turn(d_packed, cos_ref[...], -upper_ref[...], -lower_ref[...]).astype(BF)
    d_packed_ref[...] = d_packed
    d_first = dot_last(d_packed, weight_ref[:, :wide])
    xhat = high_ref[:, :model]
    inner = d_first * vector_ref[0:1] + d_second * vector_ref[2:3]
    average = jnp.mean(inner, axis=-1, keepdims=True)
    along = jnp.mean(inner * xhat, axis=-1, keepdims=True)
    total = (inner - average - xhat * along) * high_ref[:, model + hidden : model + hidden + 1]
    mine_ref[...] = total[:rows]
    other_ref[...] = total[rows:]

    def add_rows(block):
        return jnp.sum(block, axis=0, keepdims=True)

    width = sums_ref.shape[1]
    packed_sum = add_rows(d_packed.astype(F32))
    if wide < width:
        packed_sum = jnp.concatenate([packed_sum, jnp.zeros((1, width - wide), F32)], axis=1)
    sums_ref[...] = jnp.concatenate(
        [
            add_rows(d_first * xhat),
            add_rows(d_first),
            add_rows(d_second * xhat),
            add_rows(d_second),
            add_rows(grad.astype(F32)) * 0.25,
            add_rows(d_pre.astype(F32)),
            packed_sum,
            jnp.zeros((1, width), F32),
        ],
        axis=0,
    )


def weight_kernel(heads, depth, count, *refs):
    refs = list(refs)
    groups = [refs[i * 9 : (i + 1) * 9] for i in range(count)]
    terms_ref, full_refs = refs[10 * count], refs[9 * count : 10 * count]
    qkv_width = heads * 3 * HEAD
    start = heads * 4 * HEAD
    tile = terms_ref.shape[0]

    def both(index):
        return jnp.concatenate([group[index][...] for group in groups], axis=0)

    def both_grads():
        parts = []
        for group in groups:
            parts += [group[2][...], group[3][...]]
        return jnp.concatenate(parts, axis=0)

    first, second, grad = both(0), both(1), both_grads()
    d_packed, d_pre, mixed, act = both(4), both(5), both(6), both(7)
    hidden = d_pre.shape[1]
    sums = sum(group[8][...] for group in groups[1:]) + groups[0][8][...]
    full = sum(item[...] for item in full_refs[1:]) + full_refs[0][...]
    long_row = jnp.concatenate([full[6:7, :qkv_width], full[5:6, :hidden]], axis=1)
    pieces = long_row.shape[1] // depth
    stacked = jnp.concatenate(
        [long_row[:, i * depth : (i + 1) * depth] for i in range(pieces)], axis=0
    )
    stacked = jnp.concatenate([stacked] * (tile // depth), axis=1)
    rest = SMALL - 8 - pieces
    small = jnp.concatenate([sums, stacked, jnp.zeros((rest, tile), F32)], axis=0)
    terms_ref[:, :start] = jnp.concatenate(
        [dot_first(first, d_packed)[:, :qkv_width], dot_first(grad, mixed)[:, : heads * HEAD]], axis=1
    ).astype(BF)
    terms_ref[:, start : start + hidden] = dot_first(second, d_pre).astype(BF)
    terms_ref[:, start + hidden : start + 2 * hidden] = dot_first(grad, act).astype(BF)
    terms_ref[:, start + 2 * hidden :] = jnp.transpose(small).astype(BF)


def unpack_kernel(
    pipe_ref,
    own_ref,
    came_ref,
    own_small_ref,
    came_small_ref,
    qkv_ref,
    qkv_bias_ref,
    out_ref,
    fc_ref,
    fc_bias_ref,
    proj_ref,
    *vector_refs,
):
    depth = qkv_ref.shape[0]
    qkv_width, out_width = qkv_ref.shape[1] // 2, out_ref.shape[1] // 2
    hidden = fc_ref.shape[1] // 2
    start = qkv_width + out_width
    pieces = (qkv_width + hidden) // depth
    smalls = [jnp.transpose(ref[...]) for ref in (own_small_ref, came_small_ref)]
    vectors = smalls[0][:8] + smalls[1][:8]
    for index, ref in enumerate(vector_refs):
        ref[...] = vectors[index : index + 1]
    longs = [
        jnp.concatenate([small[8 + i : 9 + i] for i in range(pieces)], axis=1) for small in smalls
    ]

    def fill(lower, upper, low_bias, high_bias):
        for index, (block, bias) in enumerate(((lower, low_bias), (upper, high_bias))):
            columns = slice(index * qkv_width, (index + 1) * qkv_width)
            qkv_ref[:, columns] = block[:, :qkv_width].astype(F32)
            qkv_bias_ref[:, columns] = bias[:, :qkv_width]
            lines = slice(index * out_width, (index + 1) * out_width)
            out_ref[:, lines] = block[:, qkv_width:start].astype(F32)
            units = slice(index * hidden, (index + 1) * hidden)
            fc_ref[:, units] = block[:, start : start + hidden].astype(F32)
            fc_bias_ref[:, units] = bias[:, qkv_width:]
            proj_ref[:, units] = block[:, start + hidden : start + 2 * hidden].astype(F32)

    @pl.when(pipe_ref[0] == 0)
    def _():
        fill(own_ref, came_ref, longs[0], longs[1])

    @pl.when(pipe_ref[0] != 0)
    def _():
        fill(came_ref, own_ref, longs[1], longs[0])


def cost(flops, moved):
    return pl.CostEstimate(flops=int(flops), bytes_accessed=int(moved), transcendentals=0)


def mixed_width(heads):
    return heads * HEAD + -(heads * HEAD) % 128


def in_vmem():
    return pl.BlockSpec(memory_space=pltpu.VMEM)


def pack_call(pipe, arrays):
    qkv, out, fc = arrays[:3]
    width = (qkv.shape[1] + out.shape[1]) // 2 + fc.shape[1] + SMALL
    packet = jax.ShapeDtypeStruct((qkv.shape[0], width), BF)
    return pl.pallas_call(
        pack_kernel,
        out_shape=(packet, packet),
        in_specs=[pl.BlockSpec(memory_space=pltpu.SMEM)]
        + [pl.BlockSpec(memory_space=pl.ANY)] * len(arrays),
        scratch_shapes=[pltpu.VMEM(item.shape, item.dtype) for item in arrays]
        + [pltpu.SemaphoreType.DMA((len(arrays),))],
        compiler_params=pltpu.CompilerParams(vmem_limit_bytes=VMEM_LIMIT),
        cost_estimate=cost(0, 4e6),
        name="pack",
    )(pipe, *arrays)


def unpack_call(pipe, own, came, own_small, came_small, widths):
    depth = own.shape[0]
    qkv_width, out_width, hidden = widths
    shapes = (
        (depth, 2 * qkv_width),
        (1, 2 * qkv_width),
        (depth, 2 * out_width),
        (depth, 2 * hidden),
        (1, 2 * hidden),
        (depth, 2 * hidden),
    ) + ((1, depth),) * 5
    return pl.pallas_call(
        unpack_kernel,
        out_shape=tuple(jax.ShapeDtypeStruct(shape, F32) for shape in shapes),
        in_specs=[pl.BlockSpec(memory_space=pltpu.SMEM)] + [in_vmem()] * 4,
        compiler_params=pltpu.CompilerParams(vmem_limit_bytes=VMEM_LIMIT),
        cost_estimate=cost(0, 6e6),
        name="unpack",
    )(pipe, own, came, own_small, came_small)


def forward_call(own, far, weight, layout, heads, hidden, depth):
    rows, model = own.shape
    full = 2 * rows
    wide = layout[0].shape[1]

    def shape(height, width, kind):
        return jax.ShapeDtypeStruct((height, width), kind)

    outs = (
        shape(rows, model, F32),
        shape(rows, model, F32),
        shape(full, 2 * model + hidden + mixed_width(heads) + wide, BF),
        shape(full, model + hidden + 128, F32),
        shape(8, model, F32),
    )
    return pl.pallas_call(
        functools.partial(forward_kernel, heads, depth),
        out_shape=outs,
        compiler_params=pltpu.CompilerParams(vmem_limit_bytes=VMEM_LIMIT),
        cost_estimate=cost(4e9, 8e6),
        name="forward",
    )(own, far, weight, *layout)


def backward_call(own, far, weight, layout, kept, heads):
    rows, model = own.shape
    full = 2 * rows
    wide = layout[0].shape[1]
    low, high, vectors = kept
    hidden = high.shape[1] - model - 128
    outs = (
        jax.ShapeDtypeStruct((rows, model), F32),
        jax.ShapeDtypeStruct((rows, model), F32),
        jax.ShapeDtypeStruct((full, wide), BF),
        jax.ShapeDtypeStruct((full, hidden), BF),
        jax.ShapeDtypeStruct((8, model), F32),
    )
    return pl.pallas_call(
        functools.partial(backward_kernel, heads),
        out_shape=outs,
        compiler_params=pltpu.CompilerParams(vmem_limit_bytes=VMEM_LIMIT),
        cost_estimate=cost(5e9, 10e6),
        name="backward",
    )(own, far, weight, *layout, low, high, vectors)


def weight_call(grads, kept, backs, heads, depth):
    model = grads[0][0].shape[1]
    hidden = kept[0][1].shape[1] - model - 128
    tile = model // 2
    mixed = mixed_width(heads)
    width = heads * 4 * HEAD + 2 * hidden + SMALL
    operands, specs = [], []

    def tiled(array, first=0):
        operands.append(array)
        specs.append(pl.BlockSpec((array.shape[0], tile), lambda i: (0, first + i)))

    def part(array, start, width):
        operands.append(array)
        specs.append(pl.BlockSpec((array.shape[0], width), lambda i: (0, start // width)))

    def whole(array):
        operands.append(array)
        specs.append(pl.BlockSpec(array.shape, lambda i: (0, 0)))

    for (own, far), keep, back in zip(grads, kept, backs):
        tiled(keep[0])
        tiled(keep[0], 2)
        tiled(own)
        tiled(far)
        whole(back[2])
        whole(back[3])
        part(keep[0], 2 * model + hidden, mixed)
        part(keep[0], 2 * model, hidden)
        tiled(back[4])
    for back in backs:
        whole(back[4])
    return pl.pallas_call(
        functools.partial(weight_kernel, heads, depth, len(grads)),
        grid=(2,),
        in_specs=specs,
        out_specs=pl.BlockSpec((tile, width), lambda i: (i, 0)),
        out_shape=jax.ShapeDtypeStruct((model, width), BF),
        compiler_params=pltpu.CompilerParams(vmem_limit_bytes=VMEM_LIMIT),
        cost_estimate=cost(8e9, 10e6),
        name="weights",
    )(*operands)


def layout_of(lengths, rows, first_row, heads):
    full = 2 * rows
    ends = jnp.cumsum(lengths)
    places = (jnp.arange(full, dtype=jnp.int32) + first_row) % full
    segment = jnp.sum((places[:, None] >= ends[None, :]).astype(jnp.int32), axis=1)
    picked = segment[:, None] == jnp.arange(lengths.shape[0], dtype=jnp.int32)[None, :]
    position = places - jnp.sum(jnp.where(picked, (ends - lengths)[None, :], 0), axis=1)
    allowed = (segment[:, None] == segment[None, :]) & (places[:, None] >= places[None, :])
    bias = jnp.where(allowed, 0.0, NEG_BIG).astype(F32)
    half = ROT // 2
    inverse = jnp.exp(jnp.arange(half, dtype=F32) * (-2.0 * math.log(10000.0) / ROT))
    angles = position.astype(F32)[:, None] * inverse
    cosine, sine = jnp.cos(angles), jnp.sin(angles)
    plain = jnp.ones((full, HEAD - ROT), F32)
    empty = jnp.zeros((full, HEAD - ROT), F32)
    none = jnp.zeros((full, half), F32)
    cos_head = jnp.concatenate([cosine, cosine, plain], axis=1)
    upper_head = jnp.concatenate([-sine, none, empty], axis=1)
    lower_head = jnp.concatenate([none, sine, empty], axis=1)

    def spread(head, fill):
        rest = jnp.full((full, HEAD), fill, F32)
        table = jnp.concatenate([head, head, rest] * heads, axis=1)
        pad = -table.shape[1] % 128
        return jnp.concatenate([table, jnp.full((full, pad), fill, F32)], axis=1) if pad else table

    return spread(cos_head, 1.0), spread(upper_head, 0.0), spread(lower_head, 0.0), bias


def local(
    inputs,
    lengths,
    ln1_gain,
    ln1_shift,
    ln2_gain,
    ln2_shift,
    qkv_weight,
    qkv_bias,
    out_weight,
    fc_weight,
    fc_bias,
    proj_weight,
    branch_bias,
    cotangent,
):
    micro, rows, model = inputs.shape
    count = lax.axis_size("dp")
    pipe = lax.axis_index("pipe")
    core = lax.axis_index("tensor")
    leading = pipe == 0
    depth = qkv_weight.shape[1]
    qkv_width = qkv_weight.shape[2] // 2
    out_width = out_weight.shape[1] // 2
    hidden = fc_weight.shape[2] // 2
    heads = out_width // HEAD
    ahead_steps = count // 2

    pipe_word = pipe.astype(jnp.int32).reshape(1)
    vectors = jnp.concatenate([ln1_gain, ln1_shift, ln2_gain, ln2_shift, branch_bias], axis=0)
    vectors = jnp.pad(vectors.astype(F32), ((0, 3), (0, 0)))
    kept_part, sent_part = pack_call(
        pipe_word,
        (
            qkv_weight[0],
            jnp.transpose(out_weight[0]),
            fc_weight[0],
            jnp.transpose(proj_weight[0]),
            vectors,
            jnp.concatenate([qkv_bias, fc_bias], axis=1).astype(F32),
        ),
    )
    first_whole, second_whole = blank_call(sent_part, count), blank_call(kept_part, count)
    came_part = swap(sent_part, "pipe")
    chunk = jnp.where(leading, kept_part, came_part)
    gather = RingGather(chunk, first_whole, ahead_steps)
    later = RingGather(
        jnp.where(leading, came_part, kept_part), second_whole, count - 1 - ahead_steps
    )
    gather.advance()
    order = later.advance()
    while gather.step < gather.steps or later.step < later.steps:
        if gather.step < gather.steps:
            order = gather.advance(*order)
        if later.step < later.steps:
            order = later.advance(*order)
    weights = [gather.result(), later.result()]

    lengths = after(lengths, chunk)
    inputs, cotangent = after(inputs, sent_part), after(cotangent, chunk)
    layouts = [layout_of(lengths[m, 0], rows, core * rows, heads) for m in range(micro)]

    def complete(half, base):
        came = swap(half, "pipe")
        return (base + (half.astype(F32) + came.astype(F32))).astype(BF)

    def half_sum(mine, other):
        return (mine + swap(other, "tensor")).astype(BF)

    current = [(inputs[m], swap(inputs[m], "tensor")) for m in range(micro)]
    cotangents = [(cotangent[m], swap(cotangent[m], "tensor")) for m in range(micro)]
    stored, outputs = [], []
    for section in range(2):
        kept_rows, results = [], []
        for m in range(micro):
            own, far = current[m]
            found = forward_call(own, far, weights[section], layouts[m], heads, hidden, depth)
            kept_rows.append(found[2:])
            half = half_sum(found[0], found[1])
            base = own.astype(F32) + found[-1][4:5]
            results.append(complete(half, base))
        if section == 0:
            current = [(item, swap(item, "tensor")) for item in results]
        stored.append(kept_rows)
        outputs.append(results)

    back_outputs = [None, None]
    backs, results, halves = [], [], []
    for m in range(micro):
        own, far = cotangents[m]
        found = backward_call(own, far, weights[1], layouts[m], stored[1][m], heads)
        backs.append(found)
        halves.append(half_sum(found[0], found[1]))
        results.append(complete(halves[m], own.astype(F32)))
    back_outputs[1] = results
    grads = [(item, swap(item, "tensor")) for item in results]
    backs[-1] = (*backs[-1][:4], after(backs[-1][4], halves[-1]))
    scatter = RingScatter(weight_call(cotangents, stored[1], backs, heads, depth), ahead_steps)
    scatter.advance()
    backs, results, marks = [], [], ()
    for m in range(micro):
        own, far = grads[m]
        if marks:
            own = after(own, marks[-1])
        found = backward_call(own, far, weights[0], layouts[m], stored[0][m], heads)
        backs.append(found)
        results.append(complete(half_sum(found[0], found[1]), own.astype(F32)))
        if m + 1 < micro:
            marks = scatter.advance(found[4])
    back_outputs[0] = results
    backs[-1] = (*backs[-1][:4], after(backs[-1][4], *marks[:TIES]))
    terms = weight_call(grads, stored[0], backs, heads, depth)
    last = RingScatter(terms, count - 1 - ahead_steps)
    order = last.advance()
    while scatter.step < scatter.steps or last.step < last.steps:
        if scatter.step < scatter.steps:
            order = scatter.advance(*order[:TIES])
        if last.step < last.steps:
            order = last.advance(*order[:TIES])
    reduced = [last.result(), scatter.result()]

    activations = jnp.where(leading, jnp.stack(outputs[0]), jnp.stack(outputs[1]))[None]
    input_grads = jnp.where(leading, jnp.stack(back_outputs[0]), jnp.stack(back_outputs[1]))[None]

    start = qkv_width + out_width
    own_part = jnp.where(leading, reduced[0], reduced[1])
    given_part = jnp.where(leading, reduced[1], reduced[0])
    came_part = swap(given_part[:, : start + 2 * hidden].astype(BF), "pipe")
    smalls = jnp.concatenate(
        [own_part[:, start + 2 * hidden :], given_part[:, start + 2 * hidden :]], axis=0
    )
    lane = lax.broadcasted_iota(jnp.int32, smalls.shape, 1)
    smalls = jnp.where(lane < 8, smalls + swap(smalls, "tensor"), smalls)
    came_small = swap(smalls[depth:], "pipe")
    grads_out = unpack_call(
        pipe_word, own_part, came_part, smalls[:depth], came_small, (qkv_width, out_width, hidden)
    )
    qkv_grad, qkv_bias_grad, out_grad, fc_grad, fc_bias_grad, proj_grad = grads_out[:6]
    vector_grads = grads_out[6:]
    return (
        activations,
        input_grads,
        vector_grads[0],
        vector_grads[1],
        vector_grads[2],
        vector_grads[3],
        qkv_grad[None],
        qkv_bias_grad,
        jnp.transpose(out_grad)[None],
        fc_grad[None],
        fc_bias_grad,
        jnp.transpose(proj_grad)[None],
        vector_grads[4],
    )


def solution(mesh):
    rows = P(None, ("dp", "tensor"), None)
    vector = P("pipe", "dp")
    bias = P("pipe", "tensor")
    wide = P("pipe", "dp", "tensor")
    tall = P("pipe", "tensor", "dp")
    result = P("pipe", None, ("dp", "tensor"), None)
    return jax.shard_map(
        local,
        mesh=mesh,
        in_specs=(
            rows,
            P(None, "dp", None),
            vector,
            vector,
            vector,
            vector,
            wide,
            bias,
            tall,
            wide,
            bias,
            tall,
            vector,
            rows,
        ),
        out_specs=(
            result,
            result,
            vector,
            vector,
            vector,
            vector,
            wide,
            bias,
            tall,
            wide,
            bias,
            tall,
            vector,
        ),
        check_vma=False,
    )
```

```python
import functools
import math

import jax
import jax.numpy as jnp
from jax import lax
from jax.experimental import pallas as pl
from jax.experimental.pallas import tpu as pltpu
from jax.sharding import PartitionSpec as P

HEAD = 64
ROT = 16
EPSILON = 1e-05
NEG_BIG = -1e30
VMEM_LIMIT = 16 * 1024 * 1024
BF = jnp.bfloat16
F32 = jnp.float32
SMALL = 128
TIES = 2


def ring_device(place, count):
    if count == 8:
        return jnp.where(place < 4, 2 * place, 15 - 2 * place)
    if count == 32:
        folded = jnp.where(place < 16, place, 31 - place)
        row, column = folded // 4, folded % 4
        column = jnp.where(row % 2 == 0, column, 3 - column)
        return row * 4 + column + jnp.where(place < 16, 0, 16)
    return place


def ring_place(device, count):
    if count == 8:
        half = device // 2
        return jnp.where(device % 2 == 0, half, 7 - half)
    if count == 32:
        within = device % 16
        row, column = within // 4, within % 4
        column = jnp.where(row % 2 == 0, column, 3 - column)
        folded = row * 4 + column
        return jnp.where(device < 16, folded, 31 - folded)
    return device


def ring_list(count):
    if count == 8:
        return [0, 2, 4, 6, 7, 5, 3, 1]
    if count == 32:
        snake = []
        for row in range(4):
            line = [row * 4 + column for column in range(4)]
            snake += line if row % 2 == 0 else line[::-1]
        return snake + [16 + item for item in reversed(snake)]
    return list(range(count))


def ring_routes(count):
    order = ring_list(count)
    ahead = [(order[i], order[(i + 1) % count]) for i in range(count)]
    return ahead, [(target, source) for source, target in ahead]


def after(value, *earlier):
    return lax.optimization_barrier((value, *earlier))[0]


def tie(values, earlier):
    present = [item for item in values if item is not None]
    if not earlier or not present:
        return values
    tied = list(lax.optimization_barrier((*present, *earlier))[: len(present)])
    return [None if item is None else tied.pop(0) for item in values]


def blank_kernel(like_ref, whole_ref):
    whole_ref[:16, :] = jnp.zeros((16, whole_ref.shape[1]), whole_ref.dtype)


def blank_call(like, count):
    return pl.pallas_call(
        blank_kernel,
        out_shape=jax.ShapeDtypeStruct((count * like.shape[0], like.shape[1]), like.dtype),
        compiler_params=pltpu.CompilerParams(vmem_limit_bytes=VMEM_LIMIT),
        cost_estimate=cost(0, 1e5),
        name="blank",
    )(like)


class RingGather:
    def __init__(self, chunk, whole, forward_steps):
        self.count = lax.axis_size("dp")
        self.ahead, self.behind = ring_routes(self.count)
        self.place = ring_place(lax.axis_index("dp"), self.count)
        self.depth = chunk.shape[0]
        self.limits = (forward_steps, self.count - 1 - forward_steps)
        self.steps = max(self.limits)
        self.step = 0
        self.front = self.back = chunk
        self.whole = lax.dynamic_update_slice(
            whole, chunk, (lax.axis_index("dp") * self.depth, 0)
        )

    def put(self, block, distance):
        owner = ring_device((self.place + self.count + distance) % self.count, self.count)
        self.whole = lax.dynamic_update_slice(self.whole, block, (owner * self.depth, 0))

    def advance(self, *earlier):
        self.step += 1
        front = self.front if self.step <= self.limits[0] else None
        back = self.back if self.step <= self.limits[1] else None
        front, back = tie([front, back], earlier)
        if front is not None:
            self.front = lax.ppermute(front, "dp", self.ahead)
            self.put(self.front, -self.step)
        if back is not None:
            self.back = lax.ppermute(back, "dp", self.behind)
            self.put(self.back, self.step)
        return [item for item in (front, back) if item is not None]

    def result(self):
        while self.step < self.steps:
            self.advance()
        return self.whole


class RingScatter:
    def __init__(self, terms, forward_steps):
        self.terms = terms
        self.count = lax.axis_size("dp")
        self.place = ring_place(lax.axis_index("dp"), self.count)
        self.depth = terms.shape[0] // self.count
        self.ahead, self.behind = ring_routes(self.count)
        self.forward_steps = forward_steps
        self.backward_steps = self.count - 1 - forward_steps
        self.steps = max(self.forward_steps, self.backward_steps)
        self.step = 0
        self.front = self.back = None

    def term(self, distance):
        owner = ring_device((self.place + self.count + distance) % self.count, self.count)
        width = self.terms.shape[1]
        return lax.dynamic_slice(self.terms, (owner * self.depth, 0), (self.depth, width))

    def advance(self, *earlier):
        marks = []
        front, back = tie([self.front, self.back], earlier)
        if self.step < self.forward_steps:
            own = self.term(self.forward_steps - self.step)
            if front is not None:
                own = (own.astype(F32) + front.astype(F32)).astype(BF)
            marks.append(own)
            front = lax.ppermute(own, "dp", self.ahead)
        if self.step < self.backward_steps:
            own = self.term(self.step - self.backward_steps)
            if back is not None:
                own = (own.astype(F32) + back.astype(F32)).astype(BF)
            marks.append(own)
            back = lax.ppermute(own, "dp", self.behind)
        self.front, self.back = front, back
        self.step += 1
        return marks

    def result(self):
        while self.step < self.steps:
            self.advance()
        return self.term(0).astype(F32) + self.front.astype(F32) + self.back.astype(F32)


def swap(block, axis):
    return lax.ppermute(block, axis, [(0, 1), (1, 0)])


def dot(left, right):
    return jnp.dot(left, right, preferred_element_type=F32)


def dot_last(left, right):
    return lax.dot_general(left, right, (((1,), (1,)), ((), ())), preferred_element_type=F32)


def dot_first(left, right):
    return lax.dot_general(left, right, (((0,), (0,)), ((), ())), preferred_element_type=F32)


def softmax_rows(queries, keys, bias):
    scores = dot_last(queries, keys) * (1.0 / math.sqrt(HEAD)) + bias
    peak = jnp.max(scores, axis=-1, keepdims=True)
    expons = jnp.exp(scores - peak)
    return expons / jnp.sum(expons, axis=-1, keepdims=True)


def head_parts(packed, index):
    base = index * 3 * HEAD
    return tuple(packed[:, base + j * HEAD : base + (j + 1) * HEAD] for j in range(3))


def turn(values, cosine, upper, lower):
    width = values.shape[1]
    return (
        values * cosine
        + pltpu.roll(values, width - ROT // 2, 1) * upper
        + pltpu.roll(values, ROT // 2, 1) * lower
    )


def pack_kernel(pipe_ref, *refs):
    sources, (kept_ref, sent_ref) = refs[:5], refs[5:7]
    held, marks = refs[7:12], refs[12]
    copies = [
        pltpu.make_async_copy(source, target, marks.at[i])
        for i, (source, target) in enumerate(zip(sources, held))
    ]
    for copy in copies:
        copy.start()
    for copy in copies:
        copy.wait()
    qkv_ref, out_ref, fc_ref, proj_ref = held[:4]
    depth = qkv_ref.shape[0]
    line = held[4][...]
    rows = [line[:, i * depth : (i + 1) * depth] for i in range(5)]
    rows.append(jnp.zeros((3, depth), F32))
    long_bias = line[:, 5 * depth :]
    qkv_width, out_width = qkv_ref.shape[1] // 2, out_ref.shape[1] // 2
    hidden = fc_ref.shape[1] // 2
    start = qkv_width + out_width
    qkv_bias, fc_bias = long_bias[:, : 2 * qkv_width], long_bias[:, 2 * qkv_width :]

    def fill(target, index):
        target[:, :start] = jnp.concatenate(
            [
                qkv_ref[:, index * qkv_width : (index + 1) * qkv_width],
                out_ref[:, index * out_width : (index + 1) * out_width],
            ],
            axis=1,
        )
        target[:, start : start + hidden] = fc_ref[:, index * hidden : (index + 1) * hidden]
        target[:, start + hidden : start + 2 * hidden] = proj_ref[
            :, index * hidden : (index + 1) * hidden
        ]
        bias = jnp.concatenate(
            [
                qkv_bias[:, index * qkv_width : (index + 1) * qkv_width],
                fc_bias[:, index * hidden : (index + 1) * hidden],
            ],
            axis=1,
        )
        pieces = bias.shape[1] // depth
        small = rows + [bias[:, i * depth : (i + 1) * depth] for i in range(pieces)]
        small.append(jnp.zeros((SMALL - 8 - pieces, depth), F32))
        small = jnp.transpose(jnp.concatenate(small, axis=0))
        target[:, start + 2 * hidden :] = small.astype(BF)

    @pl.when(pipe_ref[0] == 0)
    def _():
        fill(kept_ref, 0)
        fill(sent_ref, 1)

    @pl.when(pipe_ref[0] != 0)
    def _():
        fill(kept_ref, 1)
        fill(sent_ref, 0)


def forward_kernel(
    heads,
    depth,
    own_ref,
    far_ref,
    weight_ref,
    cos_ref,
    upper_ref,
    lower_ref,
    bias_ref,
    mine_ref,
    other_ref,
    low_ref,
    high_ref,
    vector_ref,
):
    rows, model = own_ref.shape
    qkv_width = heads * 3 * HEAD
    start = heads * 4 * HEAD
    wide = cos_ref.shape[1]
    hidden = high_ref.shape[1] - model - 128
    pieces = (qkv_width + hidden) // depth
    small = jnp.transpose(weight_ref[:, start + 2 * hidden :].astype(F32))
    vectors = small[:8]
    vector_ref[...] = vectors
    long_bias = jnp.concatenate([small[8 + i : 9 + i, :depth] for i in range(pieces)], axis=1)
    qkv_bias = jnp.concatenate(
        [long_bias[:, :qkv_width], jnp.zeros((1, wide - qkv_width), F32)], axis=1
    )
    fc_bias = long_bias[:, qkv_width:]
    values = jnp.concatenate([own_ref[...], far_ref[...]], axis=0).astype(F32)
    centred = values - jnp.mean(values, axis=-1, keepdims=True)
    scale = lax.rsqrt(jnp.mean(centred * centred, axis=-1, keepdims=True) + EPSILON)
    xhat = centred * scale
    high_ref[:, :model] = xhat
    high_ref[:, model + hidden :] = jnp.broadcast_to(scale, (2 * rows, 128))
    first = (xhat * vectors[0:1] + vectors[1:2]).astype(BF)
    second = (xhat * vectors[2:3] + vectors[3:4]).astype(BF)
    low_ref[:, :model] = first
    low_ref[:, model : 2 * model] = second
    packed = dot(first, weight_ref[:, :wide]) + qkv_bias
    packed = turn(packed, cos_ref[...], upper_ref[...], lower_ref[...]).astype(BF)
    spot = low_ref.shape[1] - wide
    low_ref[:, spot:] = packed
    bias = bias_ref[...]
    mixed = []
    for index in range(heads):
        queries, keys, held = head_parts(packed, index)
        weights = softmax_rows(queries, keys, bias).astype(BF)
        mixed.append(dot(weights, held))
    mixed = jnp.concatenate(mixed, axis=1).astype(BF)
    tail = spot - 2 * model - hidden - mixed.shape[1]
    low_ref[:, 2 * model + hidden : spot] = (
        jnp.concatenate([mixed, jnp.zeros((2 * rows, tail), BF)], axis=1) if tail else mixed
    )
    pre = dot(second, weight_ref[:, start : start + hidden]) + fc_bias
    high_ref[:, model : model + hidden] = pre
    act = (pre * (0.5 + 0.5 * lax.erf(pre * math.sqrt(0.5)))).astype(BF)
    low_ref[:, 2 * model : 2 * model + hidden] = act
    total = dot_last(act, weight_ref[:, start + hidden : start + 2 * hidden])
    total = total + dot_last(mixed, weight_ref[:, qkv_width:start])
    mine_ref[...] = total[:rows]
    other_ref[...] = total[rows:]


def backward_kernel(
    heads,
    own_ref,
    far_ref,
    weight_ref,
    cos_ref,
    upper_ref,
    lower_ref,
    bias_ref,
    low_ref,
    high_ref,
    vector_ref,
    mine_ref,
    other_ref,
    d_packed_ref,
    d_pre_ref,
    sums_ref,
):
    rows, model = own_ref.shape
    qkv_width = heads * 3 * HEAD
    start = heads * 4 * HEAD
    wide = cos_ref.shape[1]
    hidden = high_ref.shape[1] - model - 128
    grad = jnp.concatenate([own_ref[...], far_ref[...]], axis=0)
    d_act = dot(grad, weight_ref[:, start + hidden : start + 2 * hidden])
    pre = high_ref[:, model : model + hidden]
    slope = 0.5 + 0.5 * lax.erf(pre * math.sqrt(0.5))
    slope = slope + pre * (jnp.exp(pre * pre * -0.5) * (1.0 / math.sqrt(2.0 * math.pi)))
    d_pre = (d_act * slope).astype(BF)
    d_pre_ref[...] = d_pre
    d_second = dot_last(d_pre, weight_ref[:, start : start + hidden])
    d_mixed = dot(grad, weight_ref[:, qkv_width:start]).astype(BF)
    bias = bias_ref[...]
    packed = low_ref[:, low_ref.shape[1] - wide :]
    parts = []
    for index in range(heads):
        queries, keys, held = head_parts(packed, index)
        weights = softmax_rows(queries, keys, bias)
        given = d_mixed[:, index * HEAD : (index + 1) * HEAD]
        d_held = dot_first(weights.astype(BF), given)
        d_weights = dot_last(given, held)
        row_dot = jnp.sum(weights * d_weights, axis=-1, keepdims=True)
        d_scores = (weights * (d_weights - row_dot)).astype(BF)
        parts.append(dot(d_scores, keys) * (1.0 / math.sqrt(HEAD)))
        parts.append(dot_first(d_scores, queries) * (1.0 / math.sqrt(HEAD)))
        parts.append(d_held)
    if wide > qkv_width:
        parts.append(jnp.zeros((2 * rows, wide - qkv_width), F32))
    d_packed = jnp.concatenate(parts, axis=1)
    d_packed = turn(d_packed, cos_ref[...], -upper_ref[...], -lower_ref[...]).astype(BF)
    d_packed_ref[...] = d_packed
    d_first = dot_last(d_packed, weight_ref[:, :wide])
    xhat = high_ref[:, :model]
    inner = d_first * vector_ref[0:1] + d_second * vector_ref[2:3]
    average = jnp.mean(inner, axis=-1, keepdims=True)
    along = jnp.mean(inner * xhat, axis=-1, keepdims=True)
    total = (inner - average - xhat * along) * high_ref[:, model + hidden : model + hidden + 1]
    mine_ref[...] = total[:rows]
    other_ref[...] = total[rows:]

    def add_rows(block):
        return jnp.sum(block, axis=0, keepdims=True)

    width = sums_ref.shape[1]
    packed_sum = add_rows(d_packed.astype(F32))
    if wide < width:
        packed_sum = jnp.concatenate([packed_sum, jnp.zeros((1, width - wide), F32)], axis=1)
    sums_ref[...] = jnp.concatenate(
        [
            add_rows(d_first * xhat),
            add_rows(d_first),
            add_rows(d_second * xhat),
            add_rows(d_second),
            add_rows(grad.astype(F32)) * 0.25,
            add_rows(d_pre.astype(F32)),
            packed_sum,
            jnp.zeros((1, width), F32),
        ],
        axis=0,
    )


def weight_kernel(heads, depth, count, *refs):
    refs = list(refs)
    groups = [refs[i * 9 : (i + 1) * 9] for i in range(count)]
    terms_ref, full_refs = refs[10 * count], refs[9 * count : 10 * count]
    qkv_width = heads * 3 * HEAD
    start = heads * 4 * HEAD
    tile = terms_ref.shape[0]

    def both(index):
        return jnp.concatenate([group[index][...] for group in groups], axis=0)

    def both_grads():
        parts = []
        for group in groups:
            parts += [group[2][...], group[3][...]]
        return jnp.concatenate(parts, axis=0)

    first, second, grad = both(0), both(1), both_grads()
    d_packed, d_pre, mixed, act = both(4), both(5), both(6), both(7)
    hidden = d_pre.shape[1]
    sums = sum(group[8][...] for group in groups[1:]) + groups[0][8][...]
    full = sum(item[...] for item in full_refs[1:]) + full_refs[0][...]
    long_row = jnp.concatenate([full[6:7, :qkv_width], full[5:6, :hidden]], axis=1)
    pieces = long_row.shape[1] // depth
    stacked = jnp.concatenate(
        [long_row[:, i * depth : (i + 1) * depth] for i in range(pieces)], axis=0
    )
    stacked = jnp.concatenate([stacked] * (tile // depth), axis=1)
    rest = SMALL - 8 - pieces
    small = jnp.concatenate([sums, stacked, jnp.zeros((rest, tile), F32)], axis=0)
    terms_ref[:, :start] = jnp.concatenate(
        [dot_first(first, d_packed)[:, :qkv_width], dot_first(grad, mixed)[:, : heads * HEAD]], axis=1
    ).astype(BF)
    terms_ref[:, start : start + hidden] = dot_first(second, d_pre).astype(BF)
    terms_ref[:, start + hidden : start + 2 * hidden] = dot_first(grad, act).astype(BF)
    terms_ref[:, start + 2 * hidden :] = jnp.transpose(small).astype(BF)


def unpack_kernel(
    pipe_ref,
    own_ref,
    came_ref,
    own_small_ref,
    came_small_ref,
    qkv_ref,
    qkv_bias_ref,
    out_ref,
    fc_ref,
    fc_bias_ref,
    proj_ref,
    *vector_refs,
):
    depth = qkv_ref.shape[0]
    qkv_width, out_width = qkv_ref.shape[1] // 2, out_ref.shape[1] // 2
    hidden = fc_ref.shape[1] // 2
    start = qkv_width + out_width
    pieces = (qkv_width + hidden) // depth
    smalls = [jnp.transpose(ref[...]) for ref in (own_small_ref, came_small_ref)]
    vectors = smalls[0][:8] + smalls[1][:8]
    for index, ref in enumerate(vector_refs):
        ref[...] = vectors[index : index + 1]
    longs = [
        jnp.concatenate([small[8 + i : 9 + i] for i in range(pieces)], axis=1) for small in smalls
    ]

    def fill(lower, upper, low_bias, high_bias):
        for index, (block, bias) in enumerate(((lower, low_bias), (upper, high_bias))):
            columns = slice(index * qkv_width, (index + 1) * qkv_width)
            qkv_ref[:, columns] = block[:, :qkv_width].astype(F32)
            qkv_bias_ref[:, columns] = bias[:, :qkv_width]
            lines = slice(index * out_width, (index + 1) * out_width)
            out_ref[:, lines] = block[:, qkv_width:start].astype(F32)
            units = slice(index * hidden, (index + 1) * hidden)
            fc_ref[:, units] = block[:, start : start + hidden].astype(F32)
            fc_bias_ref[:, units] = bias[:, qkv_width:]
            proj_ref[:, units] = block[:, start + hidden : start + 2 * hidden].astype(F32)

    @pl.when(pipe_ref[0] == 0)
    def _():
        fill(own_ref, came_ref, longs[0], longs[1])

    @pl.when(pipe_ref[0] != 0)
    def _():
        fill(came_ref, own_ref, longs[1], longs[0])


def cost(flops, moved):
    return pl.CostEstimate(flops=int(flops), bytes_accessed=int(moved), transcendentals=0)


def mixed_width(heads):
    return heads * HEAD + -(heads * HEAD) % 128


def in_vmem():
    return pl.BlockSpec(memory_space=pltpu.VMEM)


def pack_call(pipe, arrays):
    qkv, out, fc = arrays[:3]
    width = (qkv.shape[1] + out.shape[1]) // 2 + fc.shape[1] + SMALL
    packet = jax.ShapeDtypeStruct((qkv.shape[0], width), BF)
    return pl.pallas_call(
        pack_kernel,
        out_shape=(packet, packet),
        in_specs=[pl.BlockSpec(memory_space=pltpu.SMEM)]
        + [pl.BlockSpec(memory_space=pl.ANY)] * len(arrays),
        scratch_shapes=[pltpu.VMEM(item.shape, item.dtype) for item in arrays]
        + [pltpu.SemaphoreType.DMA((len(arrays),))],
        compiler_params=pltpu.CompilerParams(vmem_limit_bytes=VMEM_LIMIT),
        cost_estimate=cost(0, 4e6),
        name="pack",
    )(pipe, *arrays)


def unpack_call(pipe, own, came, own_small, came_small, widths):
    depth = own.shape[0]
    qkv_width, out_width, hidden = widths
    shapes = (
        (depth, 2 * qkv_width),
        (1, 2 * qkv_width),
        (depth, 2 * out_width),
        (depth, 2 * hidden),
        (1, 2 * hidden),
        (depth, 2 * hidden),
    ) + ((1, depth),) * 5
    return pl.pallas_call(
        unpack_kernel,
        out_shape=tuple(jax.ShapeDtypeStruct(shape, F32) for shape in shapes),
        in_specs=[pl.BlockSpec(memory_space=pltpu.SMEM)] + [in_vmem()] * 4,
        compiler_params=pltpu.CompilerParams(vmem_limit_bytes=VMEM_LIMIT),
        cost_estimate=cost(0, 6e6),
        name="unpack",
    )(pipe, own, came, own_small, came_small)


def forward_call(own, far, weight, layout, heads, hidden, depth):
    rows, model = own.shape
    full = 2 * rows
    wide = layout[0].shape[1]

    def shape(height, width, kind):
        return jax.ShapeDtypeStruct((height, width), kind)

    outs = (
        shape(rows, model, F32),
        shape(rows, model, F32),
        shape(full, 2 * model + hidden + mixed_width(heads) + wide, BF),
        shape(full, model + hidden + 128, F32),
        shape(8, model, F32),
    )
    return pl.pallas_call(
        functools.partial(forward_kernel, heads, depth),
        out_shape=outs,
        compiler_params=pltpu.CompilerParams(vmem_limit_bytes=VMEM_LIMIT),
        cost_estimate=cost(4e9, 8e6),
        name="forward",
    )(own, far, weight, *layout)


def backward_call(own, far, weight, layout, kept, heads):
    rows, model = own.shape
    full = 2 * rows
    wide = layout[0].shape[1]
    low, high, vectors = kept
    hidden = high.shape[1] - model - 128
    outs = (
        jax.ShapeDtypeStruct((rows, model), F32),
        jax.ShapeDtypeStruct((rows, model), F32),
        jax.ShapeDtypeStruct((full, wide), BF),
        jax.ShapeDtypeStruct((full, hidden), BF),
        jax.ShapeDtypeStruct((8, model), F32),
    )
    return pl.pallas_call(
        functools.partial(backward_kernel, heads),
        out_shape=outs,
        compiler_params=pltpu.CompilerParams(vmem_limit_bytes=VMEM_LIMIT),
        cost_estimate=cost(5e9, 10e6),
        name="backward",
    )(own, far, weight, *layout, low, high, vectors)


def weight_call(grads, kept, backs, heads, depth):
    model = grads[0][0].shape[1]
    hidden = kept[0][1].shape[1] - model - 128
    tile = model // 2
    mixed = mixed_width(heads)
    width = heads * 4 * HEAD + 2 * hidden + SMALL
    operands, specs = [], []

    def tiled(array, first=0):
        operands.append(array)
        specs.append(pl.BlockSpec((array.shape[0], tile), lambda i: (0, first + i)))

    def part(array, start, width):
        operands.append(array)
        specs.append(pl.BlockSpec((array.shape[0], width), lambda i: (0, start // width)))

    def whole(array):
        operands.append(array)
        specs.append(pl.BlockSpec(array.shape, lambda i: (0, 0)))

    for (own, far), keep, back in zip(grads, kept, backs):
        tiled(keep[0])
        tiled(keep[0], 2)
        tiled(own)
        tiled(far)
        whole(back[2])
        whole(back[3])
        part(keep[0], 2 * model + hidden, mixed)
        part(keep[0], 2 * model, hidden)
        tiled(back[4])
    for back in backs:
        whole(back[4])
    return pl.pallas_call(
        functools.partial(weight_kernel, heads, depth, len(grads)),
        grid=(2,),
        in_specs=specs,
        out_specs=pl.BlockSpec((tile, width), lambda i: (i, 0)),
        out_shape=jax.ShapeDtypeStruct((model, width), BF),
        compiler_params=pltpu.CompilerParams(vmem_limit_bytes=VMEM_LIMIT),
        cost_estimate=cost(8e9, 10e6),
        name="weights",
    )(*operands)


def layout_of(lengths, rows, first_row, heads):
    full = 2 * rows
    ends = jnp.cumsum(lengths)
    places = (jnp.arange(full, dtype=jnp.int32) + first_row) % full
    segment = jnp.sum((places[:, None] >= ends[None, :]).astype(jnp.int32), axis=1)
    picked = segment[:, None] == jnp.arange(lengths.shape[0], dtype=jnp.int32)[None, :]
    position = places - jnp.sum(jnp.where(picked, (ends - lengths)[None, :], 0), axis=1)
    allowed = (segment[:, None] == segment[None, :]) & (places[:, None] >= places[None, :])
    bias = jnp.where(allowed, 0.0, NEG_BIG).astype(F32)
    half = ROT // 2
    inverse = jnp.exp(jnp.arange(half, dtype=F32) * (-2.0 * math.log(10000.0) / ROT))
    angles = position.astype(F32)[:, None] * inverse
    cosine, sine = jnp.cos(angles), jnp.sin(angles)
    plain = jnp.ones((full, HEAD - ROT), F32)
    empty = jnp.zeros((full, HEAD - ROT), F32)
    none = jnp.zeros((full, half), F32)
    cos_head = jnp.concatenate([cosine, cosine, plain], axis=1)
    upper_head = jnp.concatenate([-sine, none, empty], axis=1)
    lower_head = jnp.concatenate([none, sine, empty], axis=1)

    def spread(head, fill):
        rest = jnp.full((full, HEAD), fill, F32)
        table = jnp.concatenate([head, head, rest] * heads, axis=1)
        pad = -table.shape[1] % 128
        return jnp.concatenate([table, jnp.full((full, pad), fill, F32)], axis=1) if pad else table

    return spread(cos_head, 1.0), spread(upper_head, 0.0), spread(lower_head, 0.0), bias


def local(
    inputs,
    lengths,
    ln1_gain,
    ln1_shift,
    ln2_gain,
    ln2_shift,
    qkv_weight,
    qkv_bias,
    out_weight,
    fc_weight,
    fc_bias,
    proj_weight,
    branch_bias,
    cotangent,
):
    micro, rows, model = inputs.shape
    count = lax.axis_size("dp")
    pipe = lax.axis_index("pipe")
    core = lax.axis_index("tensor")
    leading = pipe == 0
    depth = qkv_weight.shape[1]
    qkv_width = qkv_weight.shape[2] // 2
    out_width = out_weight.shape[1] // 2
    hidden = fc_weight.shape[2] // 2
    heads = out_width // HEAD
    ahead_steps = count // 2

    pipe_word = pipe.astype(jnp.int32).reshape(1)
    line = jnp.concatenate(
        [ln1_gain, ln1_shift, ln2_gain, ln2_shift, branch_bias, qkv_bias, fc_bias], axis=1
    ).astype(F32)
    kept_part, sent_part = pack_call(
        pipe_word,
        (
            qkv_weight[0],
            jnp.transpose(out_weight[0]),
            fc_weight[0],
            jnp.transpose(proj_weight[0]),
            line,
        ),
    )
    first_whole, second_whole = blank_call(sent_part, count), blank_call(kept_part, count)
    came_part = swap(sent_part, "pipe")
    chunk = jnp.where(leading, kept_part, came_part)
    gather = RingGather(chunk, first_whole, ahead_steps)
    later = RingGather(
        jnp.where(leading, came_part, kept_part), second_whole, count - 1 - ahead_steps
    )
    gather.advance()
    order = later.advance()
    while gather.step < gather.steps or later.step < later.steps:
        if gather.step < gather.steps:
            order = gather.advance(*order)
        if later.step < later.steps:
            order = later.advance(*order)
    weights = [gather.result(), later.result()]

    lengths = after(lengths, chunk)
    inputs, cotangent = after(inputs, sent_part), after(cotangent, chunk)
    layouts = [layout_of(lengths[m, 0], rows, core * rows, heads) for m in range(micro)]

    def complete(half, base):
        came = swap(half, "pipe")
        return (base + (half.astype(F32) + came.astype(F32))).astype(BF)

    def half_sum(mine, other):
        return (mine + swap(other, "tensor")).astype(BF)

    current = [(inputs[m], swap(inputs[m], "tensor")) for m in range(micro)]
    cotangents = [(cotangent[m], swap(cotangent[m], "tensor")) for m in range(micro)]
    stored, outputs = [], []
    for section in range(2):
        kept_rows, results = [], []
        for m in range(micro):
            own, far = current[m]
            found = forward_call(own, far, weights[section], layouts[m], heads, hidden, depth)
            kept_rows.append(found[2:])
            half = half_sum(found[0], found[1])
            base = own.astype(F32) + found[-1][4:5]
            results.append(complete(half, base))
        if section == 0:
            current = [(item, swap(item, "tensor")) for item in results]
        stored.append(kept_rows)
        outputs.append(results)

    back_outputs = [None, None]
    backs, results, halves = [], [], []
    for m in range(micro):
        own, far = cotangents[m]
        found = backward_call(own, far, weights[1], layouts[m], stored[1][m], heads)
        backs.append(found)
        halves.append(half_sum(found[0], found[1]))
        results.append(complete(halves[m], own.astype(F32)))
    back_outputs[1] = results
    grads = [(item, swap(item, "tensor")) for item in results]
    backs[-1] = (*backs[-1][:4], after(backs[-1][4], halves[-1]))
    scatter = RingScatter(weight_call(cotangents, stored[1], backs, heads, depth), ahead_steps)
    scatter.advance()
    backs, results, marks = [], [], ()
    for m in range(micro):
        own, far = grads[m]
        if marks:
            own = after(own, marks[-1])
        found = backward_call(own, far, weights[0], layouts[m], stored[0][m], heads)
        backs.append(found)
        results.append(complete(half_sum(found[0], found[1]), own.astype(F32)))
        if m + 1 < micro:
            marks = scatter.advance(found[4])
    back_outputs[0] = results
    backs[-1] = (*backs[-1][:4], after(backs[-1][4], *marks[:TIES]))
    terms = weight_call(grads, stored[0], backs, heads, depth)
    last = RingScatter(terms, count - 1 - ahead_steps)
    order = last.advance()
    while scatter.step < scatter.steps or last.step < last.steps:
        if scatter.step < scatter.steps:
            order = scatter.advance(*order[:TIES])
        if last.step < last.steps:
            order = last.advance(*order[:TIES])
    reduced = [last.result(), scatter.result()]

    activations = jnp.where(leading, jnp.stack(outputs[0]), jnp.stack(outputs[1]))[None]
    input_grads = jnp.where(leading, jnp.stack(back_outputs[0]), jnp.stack(back_outputs[1]))[None]

    start = qkv_width + out_width
    own_part = jnp.where(leading, reduced[0], reduced[1])
    given_part = jnp.where(leading, reduced[1], reduced[0])
    came_part = swap(given_part[:, : start + 2 * hidden].astype(BF), "pipe")
    smalls = jnp.concatenate(
        [own_part[:, start + 2 * hidden :], given_part[:, start + 2 * hidden :]], axis=0
    )
    lane = lax.broadcasted_iota(jnp.int32, smalls.shape, 1)
    smalls = jnp.where(lane < 8, smalls + swap(smalls, "tensor"), smalls)
    came_small = swap(smalls[depth:], "pipe")
    grads_out = unpack_call(
        pipe_word, own_part, came_part, smalls[:depth], came_small, (qkv_width, out_width, hidden)
    )
    qkv_grad, qkv_bias_grad, out_grad, fc_grad, fc_bias_grad, proj_grad = grads_out[:6]
    vector_grads = grads_out[6:]
    return (
        activations,
        input_grads,
        vector_grads[0],
        vector_grads[1],
        vector_grads[2],
        vector_grads[3],
        qkv_grad[None],
        qkv_bias_grad,
        jnp.transpose(out_grad)[None],
        fc_grad[None],
        fc_bias_grad,
        jnp.transpose(proj_grad)[None],
        vector_grads[4],
    )


def solution(mesh):
    rows = P(None, ("dp", "tensor"), None)
    vector = P("pipe", "dp")
    bias = P("pipe", "tensor")
    wide = P("pipe", "dp", "tensor")
    tall = P("pipe", "tensor", "dp")
    result = P("pipe", None, ("dp", "tensor"), None)
    return jax.shard_map(
        local,
        mesh=mesh,
        in_specs=(
            rows,
            P(None, "dp", None),
            vector,
            vector,
            vector,
            vector,
            wide,
            bias,
            tall,
            wide,
            bias,
            tall,
            vector,
            rows,
        ),
        out_specs=(
            result,
            result,
            vector,
            vector,
            vector,
            vector,
            wide,
            bias,
            tall,
            wide,
            bias,
            tall,
            vector,
        ),
        check_vma=False,
    )
```
